128 devices in a mesh: sta: 8 (over z, y_hi), day: 16 (over x, y_lo, core).
Axes of the slice: x: 4, y: 4 (y_hi: 2, y_lo: 2; y = y_hi * 2 + y_lo), z: 4, core: 2. Of those that a mesh axis runs over, the one named last changes fastest.
Arguments:
- spectra: bfloat16 [2, 512, 16, 4096], P(None, 'sta', 'day')
- pair_stations: int32 [1280, 2], P('sta'), may hold values from 0 to 63
Outputs:
- stacked: float32 [1280, 4096], P(('sta', 'day'))
The draws below stay inside these ranges and needn't reach their ends.
Inputs may be any that keep to these rules, and one draw needn't show every extreme that they name: `pair_stations`: in each round r of a block's rows, the first index names a station of the block and the second one of the block r below it, cyclically.
All inputs are finite; a program needn't handle non-finite values.
Results may differ from the reference program's by a relative error of at most 0.0034.
Values may be sent and summed in bfloat16 or wider, within the bound.
A program may use at most 256 MiB of HBM per device.

```python
import math
import jax
import jax.numpy as jnp
from jax import lax

BINS = 4096
LAGS = 4096
S_DEV = 64
PAIRS = 32
ROUNDS = 5
STATIONS = 512
DAYS = 16
PAIR_ROWS = 1280
N_STA = 8


def draw_spectra(key, part):
    key = jax.random.fold_in(key, 11)
    key_list = jax.random.split(key, 3)
    response = jax.random.normal(key_list[0], (2, STATIONS, 1, BINS), jnp.float32)
    source = jax.random.normal(key_list[1], (2, 1, DAYS, BINS), jnp.float32)
    noise = jax.random.normal(key_list[2], (2, STATIONS, DAYS, BINS), jnp.float32)
    real_part = response[0] * source[0] - response[1] * source[1]
    imag_part = response[0] * source[1] + response[1] * source[0]
    mixed = jnp.stack([real_part, imag_part]) + 0.8 * noise
    return mixed.astype(jnp.bfloat16)


def with_ends(values, stream_key, least, top_value):
    extent = values.shape
    spot = [jax.random.randint(jax.random.fold_in(stream_key, axis), (), 0, extent[axis]) for axis in range(len(extent))]
    values = values.at[tuple(spot)].set(least)
    longest = extent.index(max(extent))
    spot[longest] = (spot[longest] + 1) % extent[longest]
    return values.at[tuple(spot)].set(top_value)


def setup_inputs(seed: int = 0) -> dict:
    arg_keys = jax.random.split(jax.random.key(seed), 3)
    spectra = draw_spectra(jax.random.fold_in(arg_keys[2], 71), 0)
    pair_stations = with_ends(jax.random.randint(arg_keys[1], (PAIR_ROWS, 2), 0, S_DEV), jax.random.fold_in(arg_keys[1], 1), 0, S_DEV - 1).astype(jnp.int32)
    return dict(spectra=spectra, pair_stations=pair_stations)


first_bin = 36
period = 72000
floor_value = 0.25

def band_taper(bin_count):
    position = lax.iota(jnp.int32, bin_count).astype(jnp.float32) + 0.5
    ramp = 8.0 / bin_count
    return jnp.minimum(1.0, jnp.minimum(position * ramp, (bin_count - position) * ramp))

def whiten(spectra):
    values = spectra.astype(jnp.float32)
    magnitude = jnp.sqrt(values[0] * values[0] + values[1] * values[1])
    return (values / jnp.maximum(magnitude, floor_value)[None]).astype(jnp.bfloat16)

def cross_spectra(left_rows, right_rows):
    left_re = left_rows[0].astype(jnp.float32)
    left_im = left_rows[1].astype(jnp.float32)
    right_re = right_rows[0].astype(jnp.float32)
    right_im = right_rows[1].astype(jnp.float32)
    taper = band_taper(left_rows.shape[-1])
    real_part = (left_re * right_re + left_im * right_im) * taper
    imag_part = (left_im * right_re - left_re * right_im) * taper
    return jnp.concatenate([real_part, imag_part], axis=-1).astype(jnp.bfloat16)

def lag_table(bin_count, lag_count, lag_start, lag_width):
    frequency = first_bin + lax.iota(jnp.int32, bin_count)
    lag_shift = lag_start + lax.iota(jnp.int32, lag_width) - lag_count // 2
    turns = jnp.remainder(frequency[:, None] * lag_shift[None, :], period).astype(jnp.float32)
    angle = turns * (2.0 * math.pi / period)
    cosine = jnp.cos(angle)
    sine = jnp.sin(angle)
    upper_half = jnp.concatenate([cosine, sine], axis=1)
    lower_half = jnp.concatenate([-sine, cosine], axis=1)
    return jnp.concatenate([upper_half, lower_half], axis=0).astype(jnp.bfloat16)

def analytic(cross_rows, lag_count):
    bin_count = cross_rows.shape[1] // 2
    lag_width = min(512, lag_count)
    real_blocks = []
    imag_blocks = []
    for block_number in range(lag_count // lag_width):
        table = lag_table(bin_count, lag_count, block_number * lag_width, lag_width)
        result = jnp.dot(cross_rows, table, preferred_element_type=jnp.float32) * (1.0 / math.sqrt(bin_count))
        real_blocks.append(result[:, :lag_width])
        imag_blocks.append(result[:, lag_width:])
    return (jnp.concatenate(real_blocks, axis=1), jnp.concatenate(imag_blocks, axis=1))

def day_terms(cross, lag_count):
    row_count = cross.shape[0]
    day_number = cross.shape[1]
    real_part, imag_part = analytic(cross.reshape(row_count * day_number, cross.shape[2]), lag_count)
    real_part = real_part.reshape(row_count, day_number, lag_count)
    imag_part = imag_part.reshape(row_count, day_number, lag_count)
    magnitude = jnp.sqrt(real_part * real_part + imag_part * imag_part)
    denominator = jnp.maximum(magnitude, floor_value)
    return (lax.optimization_barrier(jnp.sum(real_part, axis=1)), lax.optimization_barrier(jnp.sum(real_part / denominator, axis=1)), lax.optimization_barrier(jnp.sum(imag_part / denominator, axis=1)))

def phase_stack(real_sum, phase_re, phase_im, day_count):
    linear = real_sum / day_count
    coherent_re = phase_re / day_count
    coherent_im = phase_im / day_count
    return linear * (coherent_re * coherent_re + coherent_im * coherent_im)

def reference(spectra, pair_stations):
    whitened = whiten(spectra)
    block_rows = pair_stations.reshape(N_STA, ROUNDS * PAIRS, 2)
    round_of_row = lax.iota(jnp.int32, ROUNDS * PAIRS) // PAIRS

    def one_block(inputs):
        block_index, rows_here = inputs
        left_index = (block_index * S_DEV + rows_here[:, 0]).astype(jnp.int32)
        partner = jnp.remainder(block_index - round_of_row, N_STA)
        right_index = (partner * S_DEV + rows_here[:, 1]).astype(jnp.int32)
        left_rows = jnp.take(whitened, left_index, axis=1)
        right_rows = jnp.take(whitened, right_index, axis=1)
        cross = cross_spectra(left_rows, right_rows)
        terms = day_terms(cross, LAGS)
        return phase_stack(terms[0], terms[1], terms[2], DAYS)
    stacked = lax.map(one_block, (lax.iota(jnp.int32, N_STA), block_rows))
    return stacked.reshape(N_STA * ROUNDS * PAIRS, LAGS)
```

```python
import functools
import math

import numpy as np
import jax
import jax.numpy as jnp
import ml_dtypes
from jax import lax
from jax.experimental import pallas as pl
from jax.experimental.pallas import tpu as pltpu
from jax.sharding import PartitionSpec as P

BINS = 4096
LAGS = 4096
STA = 8
DAY = 16
STATIONS = 64
ROUNDS = 5
PAIRS = 32
ROWS = ROUNDS * PAIRS
MINE = ROWS // DAY
WIDTH = BINS // STA
RANK = 64
SLOT = 16
LAG_TILE = 512
TILES = LAGS // LAG_TILE
FIRST_BIN = 36
PERIOD = 72000
MESH = pl.DeviceIdType.MESH
F32 = jnp.float32
BF16 = jnp.bfloat16


def prolate_basis(width, rank):
    t = np.arange(width, dtype=np.float64)
    half_band = LAGS / 2 / PERIOD
    diagonal = ((width - 1 - 2 * t) / 2) ** 2 * np.cos(2 * np.pi * half_band)
    off = t[1:] * (width - t[1:]) / 2
    matrix = np.diag(diagonal) + np.diag(off, 1) + np.diag(off, -1)
    _, vectors = np.linalg.eigh(matrix)
    vectors = vectors[:, ::-1][:, :rank]
    middle = width // 2
    signs = np.sign(vectors[middle])
    return vectors * signs[None]


@functools.lru_cache(maxsize=None)
def tables():
    basis = prolate_basis(WIDTH, RANK)
    lag = np.arange(LAGS, dtype=np.int64) - LAGS // 2
    rows = []
    for block in range(STA):
        bins = FIRST_BIN + block * WIDTH + np.arange(WIDTH, dtype=np.int64)
        turns = np.remainder(bins[:, None] * lag[None, :], PERIOD)
        angle = turns * (2.0 * np.pi / PERIOD)
        cosine, sine = np.cos(angle), np.sin(angle)
        rows.append(basis.T @ cosine)
        rows.append(-(basis.T @ sine))
    table = np.concatenate(rows, axis=0) / math.sqrt(BINS)
    table = table.reshape(STA * 2 * RANK, TILES, LAG_TILE).transpose(1, 0, 2)
    forward = np.zeros((2 * WIDTH, 2 * RANK))
    forward[:WIDTH, :RANK] = basis
    forward[WIDTH:, RANK:] = basis
    spread = np.zeros((DAY * SLOT, ROWS))
    for row in range(ROWS):
        spread[row // MINE * SLOT + row % MINE, row] = 1.0
    turn = np.zeros((2 * RANK, 2 * RANK))
    for i in range(RANK):
        turn[RANK + i, i] = 1.0
        turn[i, RANK + i] = -1.0
    as_bf16 = lambda a: np.ascontiguousarray(a).astype(ml_dtypes.bfloat16)
    return as_bf16(table), as_bf16(forward), as_bf16(spread), as_bf16(turn)


def dot(a, b):
    return jnp.dot(a, b, preferred_element_type=F32)


def exchange_bins(x_ref, idx_ref, w_ref, i_ref, send, isend, wsem, wrsem, isem, irsem):
    me = lax.axis_index("sta")
    barrier = pltpu.get_barrier_semaphore()
    for step in range(1, STA):
        pl.semaphore_signal(barrier, inc=1, device_id={"sta": lax.rem(me + step, STA)}, device_id_type=MESH)
    isend[...] = jnp.zeros_like(isend)
    isend[0:2, 0:ROWS] = idx_ref[...]
    for part in range(STA):
        re = x_ref[0, :, part * WIDTH : (part + 1) * WIDTH].astype(F32)
        im = x_ref[1, :, part * WIDTH : (part + 1) * WIDTH].astype(F32)
        scale = jnp.minimum(lax.rsqrt(re * re + im * im), 4.0)
        send[part, :, 0:WIDTH] = (re * scale).astype(BF16)
        send[part, :, WIDTH:] = (im * scale).astype(BF16)
    pl.semaphore_wait(barrier, STA - 1)
    copies = []
    for step in (4, 3, 5, 2, 6, 1, 7):
        to = lax.rem(me + step, STA)
        copies.append(
            pltpu.make_async_remote_copy(
                src_ref=isend, dst_ref=i_ref.at[me], send_sem=isem.at[step], recv_sem=irsem.at[step],
                device_id={"sta": to}, device_id_type=MESH,
            )
        )
        copies.append(
            pltpu.make_async_remote_copy(
                src_ref=send.at[to], dst_ref=w_ref.at[me], send_sem=wsem.at[step], recv_sem=wrsem.at[step],
                device_id={"sta": to}, device_id_type=MESH,
            )
        )
    for copy in copies:
        copy.start()
    w_ref[me] = send[me]
    i_ref[me] = isend[...]
    for copy in copies:
        copy.wait()


def coefficients(me_ref, w_ref, i_ref, forward_ref, spread_ref, y_ref, u_buf, v_buf):
    me = me_ref[0]
    lanes = lax.broadcasted_iota(jnp.int32, (ROWS, STATIONS), 1)

    def pick(block, _):
        first = jnp.transpose(i_ref[block])[0:ROWS, 0:1]
        seconds = []
        for r in range(ROUNDS):
            other = lax.rem(block + r, STA)
            seconds.append(jnp.transpose(i_ref[other])[r * PAIRS : (r + 1) * PAIRS, 1:2])
        second = jnp.concatenate(seconds, axis=0)
        hot = jnp.concatenate([first == lanes, second == lanes], axis=0)
        hot = jnp.where(hot, 1.0, 0.0).astype(BF16)
        got = dot(hot, w_ref[block]).astype(BF16)
        u_buf[block] = got[0:ROWS]
        for r in range(ROUNDS):
            v_buf[lax.rem(block + r, STA), r * PAIRS : (r + 1) * PAIRS, :] = got[ROWS + r * PAIRS : ROWS + (r + 1) * PAIRS]
        return 0

    lax.fori_loop(0, STA, pick, 0)
    position = (lax.broadcasted_iota(jnp.int32, (1, WIDTH), 1) + me * WIDTH).astype(F32) + 0.5
    ramp = 8.0 / BINS
    taper = jnp.minimum(1.0, jnp.minimum(position * ramp, (BINS - position) * ramp))

    def cross(block, _):
        ur = u_buf[block, :, 0:WIDTH].astype(F32)
        ui = u_buf[block, :, WIDTH:].astype(F32)
        vr = v_buf[block, :, 0:WIDTH].astype(F32)
        vi = v_buf[block, :, WIDTH:].astype(F32)
        cr = ((ur * vr + ui * vi) * taper).astype(BF16)
        ci = ((ui * vr - ur * vi) * taper).astype(BF16)
        y = dot(cr, forward_ref[0:WIDTH]) + dot(ci, forward_ref[WIDTH:])
        y_ref[block] = dot(spread_ref[...], y.astype(BF16)).astype(BF16)
        return 0

    lax.fori_loop(0, STA, cross, 0)


def exchange_rows(y_ref, z_ref, ssem, rsem):
    s = lax.axis_index("sta")
    d = lax.axis_index("day")
    me = s * DAY + d
    barrier = pltpu.get_barrier_semaphore()
    count = STA * DAY

    def greet(step, _):
        to = lax.rem(me + step, count)
        pl.semaphore_signal(barrier, inc=1, device_id=(to // DAY, lax.rem(to, DAY)), device_id_type=MESH)
        return 0

    lax.fori_loop(1, count, greet, 0)
    pl.semaphore_wait(barrier, count - 1)

    def push(step, _):
        to = lax.rem(me + step, count)
        pltpu.make_async_remote_copy(
            src_ref=y_ref.at[to], dst_ref=z_ref.at[me], send_sem=ssem, recv_sem=rsem,
            device_id=(to // DAY, lax.rem(to, DAY)), device_id_type=MESH,
        ).start()
        return 0

    lax.fori_loop(1, count, push, 0)
    z_ref[me] = y_ref[me]
    rest = z_ref.at[pl.ds(0, count - 1)]
    pltpu.make_async_copy(rest, rest, ssem).wait()
    pltpu.make_async_copy(rest, rest, rsem).wait()


def stack_days(z_ref, table_ref, spread_ref, turn_ref, out_ref, left, sums):
    for s in range(STA):
        rows = z_ref[s * DAY : (s + 1) * DAY].reshape(DAY * SLOT, 2 * RANK)
        packed = lax.dot_general(spread_ref[...], rows, (((0,), (0,)), ((), ())), preferred_element_type=F32).astype(BF16)
        left[0:ROWS, s * 2 * RANK : (s + 1) * 2 * RANK] = packed
        left[ROWS:, s * 2 * RANK : (s + 1) * 2 * RANK] = dot(packed, turn_ref[...]).astype(BF16)
    group = 4 * MINE

    def tile(t, _):
        both = dot(left[...], table_ref[t])
        re, im = both[0:ROWS], both[ROWS:]
        scale = jnp.minimum(lax.rsqrt(re * re + im * im), 4.0)
        parts = (re, re * scale, im * scale)
        for n, part in enumerate(parts):
            total = part[0:group]
            for g in range(1, ROWS // group):
                total = total + part[g * group : (g + 1) * group]
            sums[n] = total
        done = []
        for n in range(3):
            total = sums[n, 0:MINE, :]
            for g in range(1, 4):
                total = total + sums[n, g * MINE : (g + 1) * MINE, :]
            done.append(total * (1.0 / DAY))
        out_ref[:, pl.ds(pl.multiple_of(t * LAG_TILE, LAG_TILE), LAG_TILE)] = done[0] * (done[1] * done[1] + done[2] * done[2])
        return 0

    lax.fori_loop(0, TILES, tile, 0)


def local(spectra, pair_stations):
    table, forward, spread, turn = (jnp.asarray(a) for a in tables())
    vmem = pl.BlockSpec(memory_space=pltpu.VMEM)
    smem = pl.BlockSpec(memory_space=pltpu.SMEM)
    limit = 56 << 20
    x = spectra.reshape(2, STATIONS, BINS)
    idx = pair_stations.T
    w, i = pl.pallas_call(
        exchange_bins,
        name="exchange_bins",
        out_shape=(jax.ShapeDtypeStruct((STA, STATIONS, 2 * WIDTH), BF16), jax.ShapeDtypeStruct((STA, 8, 256), jnp.int32)),
        in_specs=[vmem, vmem],
        out_specs=(vmem, vmem),
        scratch_shapes=[
            pltpu.VMEM((STA, STATIONS, 2 * WIDTH), BF16),
            pltpu.VMEM((8, 256), jnp.int32),
            pltpu.SemaphoreType.DMA((STA,)),
            pltpu.SemaphoreType.DMA((STA,)),
            pltpu.SemaphoreType.DMA((STA,)),
            pltpu.SemaphoreType.DMA((STA,)),
        ],
        compiler_params=pltpu.CompilerParams(collective_id=0, has_side_effects=True, vmem_limit_bytes=limit),
    )(x, idx)
    me = lax.axis_index("sta").astype(jnp.int32).reshape(1)
    y = pl.pallas_call(
        coefficients,
        name="coefficients",
        out_shape=jax.ShapeDtypeStruct((STA, DAY * SLOT, 2 * RANK), BF16),
        in_specs=[smem, vmem, vmem, vmem, vmem],
        out_specs=vmem,
        scratch_shapes=[pltpu.VMEM((STA, ROWS, 2 * WIDTH), BF16)] * 2,
        compiler_params=pltpu.CompilerParams(vmem_limit_bytes=limit),
    )(me, w, i, forward, spread)
    z = pl.pallas_call(
        exchange_rows,
        name="exchange_rows",
        out_shape=jax.ShapeDtypeStruct((STA * DAY, SLOT, 2 * RANK), BF16),
        in_specs=[vmem],
        out_specs=vmem,
        scratch_shapes=[pltpu.SemaphoreType.DMA, pltpu.SemaphoreType.DMA],
        compiler_params=pltpu.CompilerParams(collective_id=1, has_side_effects=True, vmem_limit_bytes=limit),
    )(y.reshape(STA * DAY, SLOT, 2 * RANK))
    return pl.pallas_call(
        stack_days,
        name="stack_days",
        out_shape=jax.ShapeDtypeStruct((MINE, LAGS), F32),
        in_specs=[vmem] * 4,
        out_specs=vmem,
        scratch_shapes=[pltpu.VMEM((2 * ROWS, STA * 2 * RANK), BF16), pltpu.VMEM((3, 4 * MINE, LAG_TILE), F32)],
        compiler_params=pltpu.CompilerParams(vmem_limit_bytes=limit),
    )(z, table, spread, turn)


def solution(mesh):
    placed = (P(None, "sta", "day", None), P("sta", None))
    return jax.shard_map(
        local, mesh=mesh, in_specs=placed, out_specs=P(("sta", "day"), None), check_vma=False
    )
```

```python
import functools
import math

import numpy as np
import jax
import jax.numpy as jnp
import ml_dtypes
from jax import lax
from jax.experimental import pallas as pl
from jax.experimental.pallas import tpu as pltpu
from jax.sharding import PartitionSpec as P

BINS = 4096
LAGS = 4096
STA = 8
DAY = 16
STATIONS = 64
ROUNDS = 5
PAIRS = 32
ROWS = ROUNDS * PAIRS
MINE = ROWS // DAY
WIDTH = BINS // STA
RANK = 64
SLOT = 16
LAG_TILE = 512
TILES = LAGS // LAG_TILE
HALVES = 2
HALF = WIDTH // HALVES
DEVICES = STA * DAY
ORDER = (4, 3, 5, 2, 6, 1, 7)
FIRST_BIN = 36
PERIOD = 72000
MESH = pl.DeviceIdType.MESH
F32 = jnp.float32
BF16 = jnp.bfloat16


def prolate_basis(width, rank):
    t = np.arange(width, dtype=np.float64)
    half_band = LAGS / 2 / PERIOD
    diagonal = ((width - 1 - 2 * t) / 2) ** 2 * np.cos(2 * np.pi * half_band)
    off = t[1:] * (width - t[1:]) / 2
    matrix = np.diag(diagonal) + np.diag(off, 1) + np.diag(off, -1)
    _, vectors = np.linalg.eigh(matrix)
    vectors = vectors[:, ::-1][:, :rank]
    middle = width // 2
    signs = np.sign(vectors[middle])
    return vectors * signs[None]


@functools.lru_cache(maxsize=None)
def tables():
    basis = prolate_basis(WIDTH, RANK)
    lag = np.arange(LAGS, dtype=np.int64) - LAGS // 2
    rows = []
    for block in range(STA):
        bins = FIRST_BIN + block * WIDTH + np.arange(WIDTH, dtype=np.int64)
        turns = np.remainder(bins[:, None] * lag[None, :], PERIOD)
        angle = turns * (2.0 * np.pi / PERIOD)
        cosine, sine = np.cos(angle), np.sin(angle)
        rows.append(basis.T @ cosine)
        rows.append(-(basis.T @ sine))
    table = np.concatenate(rows, axis=0) / math.sqrt(BINS)
    table = table.reshape(STA * 2 * RANK, TILES, LAG_TILE).transpose(1, 0, 2)
    high = basis.astype(ml_dtypes.bfloat16).astype(np.float64)
    forward = np.zeros((HALVES, 2, HALF, 4, RANK))
    for half in range(HALVES):
        rows = slice(half * HALF, (half + 1) * HALF)
        for n, part in enumerate((high, basis - high)):
            forward[half, 0, :, 2 * n] = part[rows]
            forward[half, 1, :, 2 * n + 1] = part[rows]
    forward = forward.reshape(HALVES, 2 * HALF, 4 * RANK)
    spread = np.zeros((DAY * SLOT, ROWS))
    for row in range(ROWS):
        spread[row // MINE * SLOT + row % MINE, row] = 1.0
    as_bf16 = lambda a: np.ascontiguousarray(a).astype(ml_dtypes.bfloat16)
    return as_bf16(table), as_bf16(forward), as_bf16(spread)


def dot(a, b):
    return jnp.dot(a, b, preferred_element_type=F32)


def correlate(x_ref, idx_ref, forward_ref, spread_ref, table_hbm, out_ref,
              send, recv, isend, irecv, hot, u_buf, v_buf, y_sum, y_buf, z_buf, left, sums, table,
              wsem, wrsem, isem, irsem, tsem, ssem, rsem):
    s = lax.axis_index("sta")
    d = lax.axis_index("day")
    me = s * DAY + d

    barrier = pltpu.get_barrier_semaphore()
    for step in range(1, STA):
        pl.semaphore_signal(barrier, inc=1, device_id=(lax.rem(s + step, STA), d), device_id_type=MESH)
    for step in range(1, DAY):
        pl.semaphore_signal(barrier, inc=1, device_id=(s, lax.rem(d + step, DAY)), device_id_type=MESH)

    def whiten(half):
        for part in range(STA):
            at = part * WIDTH + half * HALF
            re = x_ref[0, :, at : at + HALF].astype(F32)
            im = x_ref[1, :, at : at + HALF].astype(F32)
            scale = jnp.minimum(lax.rsqrt(re * re + im * im), 4.0)
            send[half, part, :, 0:HALF] = (re * scale).astype(BF16)
            send[half, part, :, HALF:] = (im * scale).astype(BF16)

    def bins_copy(half, step):
        to = lax.rem(s + step, STA)
        return pltpu.make_async_remote_copy(
            src_ref=send.at[half, to], dst_ref=recv.at[half, s],
            send_sem=wsem.at[half, step], recv_sem=wrsem.at[half, step],
            device_id=(to, d), device_id_type=MESH,
        )

    def pairs_copy(step):
        return pltpu.make_async_remote_copy(
            src_ref=isend, dst_ref=irecv.at[s], send_sem=isem.at[step], recv_sem=irsem.at[step],
            device_id=(lax.rem(s + step, STA), d), device_id_type=MESH,
        )

    def table_copy(t):
        return pltpu.make_async_copy(table_hbm.at[t], table.at[t], tsem.at[t])

    isend[...] = jnp.zeros_like(isend)
    isend[0:2, 0:ROWS] = idx_ref[...]
    whiten(0)
    pl.semaphore_wait(barrier, STA + DAY - 2)
    for step in ORDER:
        pairs_copy(step).start()
    for step in ORDER:
        bins_copy(0, step).start()
    for half in range(1, HALVES):
        whiten(half)
        for step in ORDER:
            bins_copy(half, step).start()
    for t in range(TILES):
        table_copy(t).start()
    for half in range(HALVES):
        recv[half, s] = send[half, s]
    irecv[s] = isend[...]

    for step in ORDER:
        pairs_copy(step).wait()
    lanes = lax.broadcasted_iota(jnp.int32, (ROWS, STATIONS), 1)

    def choose(block, _):
        rows = jnp.transpose(irecv[block])
        hot[block, 0:ROWS] = jnp.where(rows[0:ROWS, 0:1] == lanes, 1.0, 0.0).astype(BF16)
        second = jnp.where(rows[0:ROWS, 1:2] == lanes, 1.0, 0.0).astype(BF16)
        for r in range(ROUNDS):
            partner = lax.rem(block - r + STA, STA)
            hot[partner, ROWS + r * PAIRS : ROWS + (r + 1) * PAIRS] = second[r * PAIRS : (r + 1) * PAIRS]
        return 0

    lax.fori_loop(0, STA, choose, 0)
    ramp = 8.0 / BINS

    for half in range(HALVES):
        for step in ORDER:
            bins_copy(half, step).wait()

        def pick(block, _):
            got = dot(hot[block], recv[half, block])
            u_buf[block] = got[0:ROWS]
            for r in range(ROUNDS):
                at = r * PAIRS
                v_buf[lax.rem(block + r, STA), at : at + PAIRS, :] = got[ROWS + at : ROWS + at + PAIRS]
            return 0

        lax.fori_loop(0, STA, pick, 0)
        start = s * WIDTH + half * HALF
        position = (lax.broadcasted_iota(jnp.int32, (1, HALF), 1) + start).astype(F32) + 0.5
        taper = jnp.minimum(1.0, jnp.minimum(position * ramp, (BINS - position) * ramp))

        def cross(n, _):
            block = lax.rem(s + 1 + n, STA)
            ur, ui = u_buf[block, :, 0:HALF], u_buf[block, :, HALF:]
            vr, vi = v_buf[block, :, 0:HALF], v_buf[block, :, HALF:]
            cr = ((ur * vr + ui * vi) * taper).astype(BF16)
            ci = ((ui * vr - ur * vi) * taper).astype(BF16)
            both = dot(jnp.concatenate([cr, ci], axis=1), forward_ref[half])
            y = both[:, 0 : 2 * RANK] + both[:, 2 * RANK :]
            if half > 0:
                y = y + y_sum[block]
            if half < HALVES - 1:
                y_sum[block] = y
                return 0
            rows = dot(spread_ref[...], y.astype(BF16)).astype(BF16)
            y_buf[pl.ds(block * DAY, DAY)] = rows.reshape(DAY, SLOT, 2 * RANK)

            def push(to, _):
                @pl.when(block * DAY + to != me)
                def _():
                    pltpu.make_async_remote_copy(
                        src_ref=y_buf.at[block * DAY + to], dst_ref=z_buf.at[me], send_sem=ssem, recv_sem=rsem,
                        device_id=(block, to), device_id_type=MESH,
                    ).start()
                return 0

            lax.fori_loop(0, DAY, push, 0)
            return 0

        lax.fori_loop(0, STA, cross, 0)

    z_buf[me] = y_buf[me]
    for t in range(TILES):
        table_copy(t).wait()
    rest = z_buf.at[pl.ds(0, DEVICES - 1)]
    pltpu.make_async_copy(rest, rest, ssem).wait()
    pltpu.make_async_copy(rest, rest, rsem).wait()

    sign = jnp.where(lax.broadcasted_iota(jnp.int32, (1, 2 * RANK), 1) < RANK, 1.0, -1.0)
    for block in range(STA):
        rows = z_buf[block * DAY : (block + 1) * DAY].reshape(DAY * SLOT, 2 * RANK)
        packed = lax.dot_general(spread_ref[...], rows, (((0,), (0,)), ((), ())), preferred_element_type=F32)
        at = block * 2 * RANK
        left[0:ROWS, at : at + 2 * RANK] = packed.astype(BF16)
        left[ROWS:, at : at + 2 * RANK] = (pltpu.roll(packed, RANK, 1) * sign).astype(BF16)
    group = 4 * MINE

    def tile(t, _):
        both = dot(left[...], table[t])
        re, im = both[0:ROWS], both[ROWS:]
        scale = jnp.minimum(lax.rsqrt(re * re + im * im), 4.0)
        for n, part in enumerate((re, re * scale, im * scale)):
            total = part[0:group]
            for g in range(1, ROWS // group):
                total = total + part[g * group : (g + 1) * group]
            sums[n] = total
        done = []
        for n in range(3):
            total = sums[n, 0:MINE, :]
            for g in range(1, 4):
                total = total + sums[n, g * MINE : (g + 1) * MINE, :]
            done.append(total * (1.0 / DAY))
        lags = pl.ds(pl.multiple_of(t * LAG_TILE, LAG_TILE), LAG_TILE)
        out_ref[:, lags] = done[0] * (done[1] * done[1] + done[2] * done[2])
        return 0

    lax.fori_loop(0, TILES, tile, 0)


def local(spectra, pair_stations):
    table, forward, spread = (jnp.asarray(a) for a in tables())
    vmem = pl.BlockSpec(memory_space=pltpu.VMEM)
    dma = pltpu.SemaphoreType.DMA
    return pl.pallas_call(
        correlate,
        name="correlate",
        out_shape=jax.ShapeDtypeStruct((MINE, LAGS), F32),
        in_specs=[vmem, vmem, vmem, vmem, pl.BlockSpec(memory_space=pl.ANY)],
        out_specs=vmem,
        scratch_shapes=[
            pltpu.VMEM((HALVES, STA, STATIONS, 2 * HALF), BF16),
            pltpu.VMEM((HALVES, STA, STATIONS, 2 * HALF), BF16),
            pltpu.VMEM((8, 256), jnp.int32),
            pltpu.VMEM((STA, 8, 256), jnp.int32),
            pltpu.VMEM((STA, 2 * ROWS, STATIONS), BF16),
            pltpu.VMEM((STA, ROWS, 2 * HALF), F32),
            pltpu.VMEM((STA, ROWS, 2 * HALF), F32),
            pltpu.VMEM((STA, ROWS, 2 * RANK), F32),
            pltpu.VMEM((DEVICES, SLOT, 2 * RANK), BF16),
            pltpu.VMEM((DEVICES, SLOT, 2 * RANK), BF16),
            pltpu.VMEM((2 * ROWS, STA * 2 * RANK), BF16),
            pltpu.VMEM((3, 4 * MINE, LAG_TILE), F32),
            pltpu.VMEM((TILES, STA * 2 * RANK, LAG_TILE), BF16),
            dma((HALVES, STA)),
            dma((HALVES, STA)),
            dma((STA,)),
            dma((STA,)),
            dma((TILES,)),
            dma,
            dma,
        ],
        compiler_params=pltpu.CompilerParams(collective_id=0, has_side_effects=True, vmem_limit_bytes=56 << 20),
    )(spectra.reshape(2, STATIONS, BINS), pair_stations.T, forward, spread, table)


def solution(mesh):
    placed = (P(None, "sta", "day", None), P("sta", None))
    return jax.shard_map(
        local, mesh=mesh, in_specs=placed, out_specs=P(("sta", "day"), None), check_vma=False
    )
```

```python
import functools
import math

import numpy as np
import jax
import jax.numpy as jnp
import ml_dtypes
from jax import lax
from jax.experimental import pallas as pl
from jax.experimental.pallas import tpu as pltpu
from jax.sharding import PartitionSpec as P

BINS = 4096
LAGS = 4096
STA = 8
DAY = 16
STATIONS = 64
ROUNDS = 5
PAIRS = 32
ROWS = ROUNDS * PAIRS
MINE = ROWS // DAY
WIDTH = BINS // STA
RANK = 64
SLOT = 16
LAG_TILE = 512
TILES = LAGS // LAG_TILE
HALVES = 2
HALF = WIDTH // HALVES
DEVICES = STA * DAY
STEPS = range(1, STA)
FIRST_BIN = 36
PERIOD = 72000
MESH = pl.DeviceIdType.MESH
F32 = jnp.float32
BF16 = jnp.bfloat16


def prolate_basis(width, rank):
    t = np.arange(width, dtype=np.float64)
    half_band = LAGS / 2 / PERIOD
    diagonal = ((width - 1 - 2 * t) / 2) ** 2 * np.cos(2 * np.pi * half_band)
    off = t[1:] * (width - t[1:]) / 2
    matrix = np.diag(diagonal) + np.diag(off, 1) + np.diag(off, -1)
    _, vectors = np.linalg.eigh(matrix)
    vectors = vectors[:, ::-1][:, :rank]
    middle = width // 2
    signs = np.sign(vectors[middle])
    return vectors * signs[None]


@functools.lru_cache(maxsize=None)
def tables():
    basis = prolate_basis(WIDTH, RANK)
    lag = np.arange(LAGS, dtype=np.int64) - LAGS // 2
    rows = []
    for block in range(STA):
        bins = FIRST_BIN + block * WIDTH + np.arange(WIDTH, dtype=np.int64)
        turns = np.remainder(bins[:, None] * lag[None, :], PERIOD)
        angle = turns * (2.0 * np.pi / PERIOD)
        cosine, sine = np.cos(angle), np.sin(angle)
        rows.append(basis.T @ cosine)
        rows.append(-(basis.T @ sine))
    table = np.concatenate(rows, axis=0) / math.sqrt(BINS)
    table = table.reshape(STA * 2 * RANK, TILES, LAG_TILE).transpose(1, 0, 2)
    high = basis.astype(ml_dtypes.bfloat16).astype(np.float64)
    forward = np.zeros((HALVES, 2, HALF, 4, RANK))
    for half in range(HALVES):
        rows = slice(half * HALF, (half + 1) * HALF)
        for n, part in enumerate((high, basis - high)):
            forward[half, 0, :, 2 * n] = part[rows]
            forward[half, 1, :, 2 * n + 1] = part[rows]
    forward = forward.reshape(HALVES, 2 * HALF, 4 * RANK)
    spread = np.zeros((DAY * SLOT, ROWS))
    for row in range(ROWS):
        spread[row // MINE * SLOT + row % MINE, row] = 1.0
    as_bf16 = lambda a: np.ascontiguousarray(a).astype(ml_dtypes.bfloat16)
    return as_bf16(table), as_bf16(forward), as_bf16(spread), as_bf16(spread.T)


def dot(a, b):
    return jnp.dot(a, b, preferred_element_type=F32)


def correlate(x_hbm, idx_hbm, forward_hbm, spread_hbm, gather_hbm, table_hbm, out_ref,
              recv, pairs, hot, u_buf, v_buf, y_sum, y_buf, z_buf, left, sums, forward, spread, gather, table,
              wsem, wrsem, isem, irsem, osem, csem, tsem, ssem, rsem):
    s = lax.axis_index("sta")
    d = lax.axis_index("day")
    me = s * DAY + d

    barrier = pltpu.get_barrier_semaphore()
    for step in STEPS:
        pl.semaphore_signal(barrier, inc=1, device_id=(lax.rem(s + step, STA), d), device_id_type=MESH)
    for step in range(1, DAY):
        pl.semaphore_signal(barrier, inc=1, device_id=(s, lax.rem(d + step, DAY)), device_id_type=MESH)

    def bins_of(part, half):
        at = pl.multiple_of(part * WIDTH + half * HALF, HALF)
        return x_hbm.at[:, :, pl.ds(at, HALF)]

    def bins_copy(half, step):
        to = lax.rem(s + step, STA)
        return pltpu.make_async_remote_copy(
            src_ref=bins_of(to, half), dst_ref=recv.at[half, step],
            send_sem=wsem.at[half, step], recv_sem=wrsem.at[half, step],
            device_id=(to, d), device_id_type=MESH,
        )

    def pairs_copy(step):
        return pltpu.make_async_remote_copy(
            src_ref=idx_hbm, dst_ref=pairs.at[step], send_sem=isem.at[step], recv_sem=irsem.at[step],
            device_id=(lax.rem(s + step, STA), d), device_id_type=MESH,
        )

    own = [pltpu.make_async_copy(bins_of(s, half), recv.at[half, 0], osem.at[half]) for half in range(HALVES)]
    own.append(pltpu.make_async_copy(idx_hbm, pairs.at[0], osem.at[HALVES]))
    constants = [
        pltpu.make_async_copy(a, b, csem.at[n])
        for n, (a, b) in enumerate(((forward_hbm, forward), (spread_hbm, spread), (gather_hbm, gather)))
    ]
    tables_in = [pltpu.make_async_copy(table_hbm.at[t], table.at[t], tsem.at[t]) for t in range(TILES)]

    for copy in own:
        copy.start()
    pl.semaphore_wait(barrier, STA + DAY - 2)
    for step in STEPS:
        pairs_copy(step).start()
    for half in range(HALVES):
        for step in STEPS:
            bins_copy(half, step).start()
    for copy in constants + tables_in:
        copy.start()

    for step in STEPS:
        pairs_copy(step).wait()
    own[HALVES].wait()
    lanes = lax.broadcasted_iota(jnp.int32, (ROWS, STATIONS), 1)
    blank = jnp.zeros((8 - 2, ROWS), jnp.int32)
    for block in range(STA):
        rows = jnp.transpose(jnp.concatenate([pairs[block], blank], axis=0))
        hot[block, 0:ROWS] = jnp.where(rows[:, 0:1] == lanes, 1.0, 0.0).astype(BF16)
        second = jnp.where(rows[:, 1:2] == lanes, 1.0, 0.0).astype(BF16)
        for r in range(ROUNDS):
            at = r * PAIRS
            hot[(block + r) % STA, ROWS + at : ROWS + at + PAIRS] = second[at : at + PAIRS]
    for copy in constants:
        copy.wait()

    def pick(half, block):
        re = recv[half, block, 0].astype(F32)
        im = recv[half, block, 1].astype(F32)
        scale = jnp.minimum(lax.rsqrt(re * re + im * im), 4.0)
        for n, part in enumerate((re, im)):
            got = dot(hot[block], (part * scale).astype(BF16))
            u_buf[block, n] = got[0:ROWS]
            for r in range(ROUNDS):
                at = r * PAIRS
                v_buf[(block - r) % STA, n, at : at + PAIRS] = got[ROWS + at : ROWS + at + PAIRS]

    def cross(half, block, taper):
        ur, ui, vr, vi = u_buf[block, 0], u_buf[block, 1], v_buf[block, 0], v_buf[block, 1]
        cr = ((ur * vr + ui * vi) * taper).astype(BF16)
        ci = ((ui * vr - ur * vi) * taper).astype(BF16)
        both = dot(jnp.concatenate([cr, ci], axis=1), forward[half])
        y = both[:, 0 : 2 * RANK] + both[:, 2 * RANK :]
        if half > 0:
            y = y + y_sum[block]
        if half < HALVES - 1:
            y_sum[block] = y
        else:
            rows = dot(spread[...], y.astype(BF16)).astype(BF16)
            y_buf[block] = rows.reshape(DAY, SLOT, 2 * RANK)

    def push(block):
        other = lax.rem(s - block + STA, STA)
        for step in range(DAY):
            if block == 0 and step == 0:
                continue
            to = lax.rem(d + step, DAY)
            pltpu.make_async_remote_copy(
                src_ref=y_buf.at[block, to], dst_ref=z_buf.at[me], send_sem=ssem, recv_sem=rsem,
                device_id=(other, to), device_id_type=MESH,
            ).start()

    ramp = 8.0 / BINS
    for half in range(HALVES):
        for step in STEPS:
            bins_copy(half, step).wait()
        own[half].wait()
        for block in range(STA):
            pick(half, block)
        start = s * WIDTH + half * HALF
        position = (lax.broadcasted_iota(jnp.int32, (1, HALF), 1) + start).astype(F32) + 0.5
        taper = jnp.minimum(1.0, jnp.minimum(position * ramp, (BINS - position) * ramp))
        order = [n % STA for n in range(1, STA + 1)]
        for n, block in enumerate(order):
            cross(half, block, taper)
            if half == HALVES - 1 and n > 0:
                push(order[n - 1])
    push(order[-1])
    z_buf[me] = y_buf[0, d]

    for copy in tables_in:
        copy.wait()
    rest = z_buf.at[pl.ds(0, DEVICES - 1)]
    pltpu.make_async_copy(rest, rest, ssem).wait()
    pltpu.make_async_copy(rest, rest, rsem).wait()

    sign = jnp.where(lax.broadcasted_iota(jnp.int32, (1, 2 * RANK), 1) < RANK, 1.0, -1.0)
    for block in range(0, STA, 2):
        rows = [z_buf[n * DAY : (n + 1) * DAY].reshape(DAY * SLOT, 2 * RANK) for n in (block, block + 1)]
        packed = dot(gather[...], jnp.concatenate(rows, axis=1))
        for n in range(2):
            part = packed[:, n * 2 * RANK : (n + 1) * 2 * RANK]
            at = (block + n) * 2 * RANK
            left[0:ROWS, at : at + 2 * RANK] = part.astype(BF16)
            left[ROWS:, at : at + 2 * RANK] = (pltpu.roll(part, RANK, 1) * sign).astype(BF16)
    group = 4 * MINE

    for t in range(TILES):
        both = dot(left[...], table[t])
        re, im = both[0:ROWS], both[ROWS:]
        scale = jnp.minimum(lax.rsqrt(re * re + im * im), 4.0)
        done = []
        for n, part in enumerate((re, re * scale, im * scale)):
            total = part[0:group]
            for g in range(1, ROWS // group):
                total = total + part[g * group : (g + 1) * group]
            sums[t % 2, n] = total
            total = sums[t % 2, n, 0:MINE]
            for g in range(1, 4):
                total = total + sums[t % 2, n, g * MINE : (g + 1) * MINE]
            done.append(total * (1.0 / DAY))
        out_ref[:, t * LAG_TILE : (t + 1) * LAG_TILE] = done[0] * (done[1] * done[1] + done[2] * done[2])


def local(spectra, pair_stations):
    table, forward, spread, gather = (jnp.asarray(a) for a in tables())
    anywhere = pl.BlockSpec(memory_space=pl.ANY)
    dma = pltpu.SemaphoreType.DMA
    return pl.pallas_call(
        correlate,
        name="correlate",
        out_shape=jax.ShapeDtypeStruct((MINE, LAGS), F32),
        in_specs=[anywhere] * 6,
        out_specs=pl.BlockSpec(memory_space=pltpu.VMEM),
        scratch_shapes=[
            pltpu.VMEM((HALVES, STA, 2, STATIONS, HALF), BF16),
            pltpu.VMEM((STA, 2, ROWS), jnp.int32),
            pltpu.VMEM((STA, 2 * ROWS, STATIONS), BF16),
            pltpu.VMEM((STA, 2, ROWS, HALF), F32),
            pltpu.VMEM((STA, 2, ROWS, HALF), F32),
            pltpu.VMEM((STA, ROWS, 2 * RANK), F32),
            pltpu.VMEM((STA, DAY, SLOT, 2 * RANK), BF16),
            pltpu.VMEM((DEVICES, SLOT, 2 * RANK), BF16),
            pltpu.VMEM((2 * ROWS, STA * 2 * RANK), BF16),
            pltpu.VMEM((2, 3, 4 * MINE, LAG_TILE), F32),
            pltpu.VMEM((HALVES, 2 * HALF, 4 * RANK), BF16),
            pltpu.VMEM((DAY * SLOT, ROWS), BF16),
            pltpu.VMEM((ROWS, DAY * SLOT), BF16),
            pltpu.VMEM((TILES, STA * 2 * RANK, LAG_TILE), BF16),
            dma((HALVES, STA)),
            dma((HALVES, STA)),
            dma((STA,)),
            dma((STA,)),
            dma((HALVES + 1,)),
            dma((3,)),
            dma((TILES,)),
            dma,
            dma,
        ],
        compiler_params=pltpu.CompilerParams(collective_id=0, has_side_effects=True, vmem_limit_bytes=56 << 20),
    )(spectra.reshape(2, STATIONS, BINS), pair_stations.T, forward, spread, gather, table)


def solution(mesh):
    placed = (P(None, "sta", "day", None), P("sta", None))
    return jax.shard_map(
        local, mesh=mesh, in_specs=placed, out_specs=P(("sta", "day"), None), check_vma=False
    )
```

```python
import functools
import math

import numpy as np
import jax
import jax.numpy as jnp
import ml_dtypes
from jax import lax
from jax.experimental import pallas as pl
from jax.experimental.pallas import tpu as pltpu
from jax.sharding import PartitionSpec as P

BINS = 4096
LAGS = 4096
STA = 8
DAY = 16
STATIONS = 64
ROUNDS = 5
PAIRS = 32
ROWS = ROUNDS * PAIRS
MINE = ROWS // DAY
WIDTH = BINS // STA
RANK = 64
SLOT = 16
LAG_TILE = 512
TILES = LAGS // LAG_TILE
CHUNKS = (384, 128)
HALVES = len(CHUNKS)
STARTS = tuple(sum(CHUNKS[:n]) for n in range(HALVES))
DEVICES = STA * DAY
STEPS = range(1, STA)
FIRST_BIN = 36
PERIOD = 72000
MESH = pl.DeviceIdType.MESH
F32 = jnp.float32
BF16 = jnp.bfloat16


def prolate_basis(width, rank):
    t = np.arange(width, dtype=np.float64)
    half_band = LAGS / 2 / PERIOD
    diagonal = ((width - 1 - 2 * t) / 2) ** 2 * np.cos(2 * np.pi * half_band)
    off = t[1:] * (width - t[1:]) / 2
    matrix = np.diag(diagonal) + np.diag(off, 1) + np.diag(off, -1)
    _, vectors = np.linalg.eigh(matrix)
    vectors = vectors[:, ::-1][:, :rank]
    middle = width // 2
    signs = np.sign(vectors[middle])
    return vectors * signs[None]


@functools.lru_cache(maxsize=None)
def tables():
    basis = prolate_basis(WIDTH, RANK)
    lag = np.arange(LAGS, dtype=np.int64) - LAGS // 2
    rows = []
    for block in range(STA):
        bins = FIRST_BIN + block * WIDTH + np.arange(WIDTH, dtype=np.int64)
        turns = np.remainder(bins[:, None] * lag[None, :], PERIOD)
        angle = turns * (2.0 * np.pi / PERIOD)
        cosine, sine = np.cos(angle), np.sin(angle)
        rows.append(basis.T @ cosine)
        rows.append(-(basis.T @ sine))
    table = np.concatenate(rows, axis=0) / math.sqrt(BINS)
    table = table.reshape(STA * 2 * RANK, TILES, LAG_TILE).transpose(1, 0, 2)
    high = basis.astype(ml_dtypes.bfloat16).astype(np.float64)
    forward = []
    for start, width in zip(STARTS, CHUNKS):
        piece = np.zeros((2, width, 4, RANK))
        for n, part in enumerate((high, basis - high)):
            piece[0, :, 2 * n] = part[start : start + width]
            piece[1, :, 2 * n + 1] = part[start : start + width]
        forward.append(piece.reshape(2 * width, 4 * RANK))
    forward = np.concatenate(forward, axis=0)
    spread = np.zeros((DAY * SLOT, ROWS))
    for row in range(ROWS):
        spread[row // MINE * SLOT + row % MINE, row] = 1.0
    as_bf16 = lambda a: np.ascontiguousarray(a).astype(ml_dtypes.bfloat16)
    return as_bf16(table), as_bf16(forward), as_bf16(spread), as_bf16(spread.T)


def dot(a, b):
    return jnp.dot(a, b, preferred_element_type=F32)


def correlate(x_hbm, idx_hbm, forward_hbm, spread_hbm, gather_hbm, table_hbm, out_ref,
              recv, pairs, hot, u_buf, v_buf, y_sum, y_buf, z_buf, left, sums, forward, spread, gather, table,
              wsem, wrsem, isem, irsem, osem, csem, tsem, ssem, rsem):
    s = lax.axis_index("sta")
    d = lax.axis_index("day")
    me = s * DAY + d

    barrier = pltpu.get_barrier_semaphore()
    for step in STEPS:
        pl.semaphore_signal(barrier, inc=1, device_id=(lax.rem(s + step, STA), d), device_id_type=MESH)
    for step in range(1, DAY):
        pl.semaphore_signal(barrier, inc=1, device_id=(s, lax.rem(d + step, DAY)), device_id_type=MESH)

    def bins_of(part, half):
        at = pl.multiple_of(part * WIDTH + STARTS[half], 128)
        return x_hbm.at[:, :, pl.ds(at, CHUNKS[half])]

    def landing(half, block):
        return recv.at[block, :, :, STARTS[half] : STARTS[half] + CHUNKS[half]]

    def bins_copy(half, step):
        to = lax.rem(s + step, STA)
        return pltpu.make_async_remote_copy(
            src_ref=bins_of(to, half), dst_ref=landing(half, step),
            send_sem=wsem.at[half, step], recv_sem=wrsem.at[half, step],
            device_id=(to, d), device_id_type=MESH,
        )

    def pairs_copy(step):
        return pltpu.make_async_remote_copy(
            src_ref=idx_hbm, dst_ref=pairs.at[step], send_sem=isem.at[step], recv_sem=irsem.at[step],
            device_id=(lax.rem(s + step, STA), d), device_id_type=MESH,
        )

    own = [pltpu.make_async_copy(bins_of(s, half), landing(half, 0), osem.at[half]) for half in range(HALVES)]
    own.append(pltpu.make_async_copy(idx_hbm, pairs.at[0], osem.at[HALVES]))
    constants = [
        pltpu.make_async_copy(a, b, csem.at[n])
        for n, (a, b) in enumerate(((forward_hbm, forward), (spread_hbm, spread), (gather_hbm, gather)))
    ]
    tables_in = [pltpu.make_async_copy(table_hbm.at[t], table.at[t], tsem.at[t]) for t in range(TILES)]

    for copy in own:
        copy.start()
    pl.semaphore_wait(barrier, STA + DAY - 2)
    for step in STEPS:
        pairs_copy(step).start()
    for half in range(HALVES):
        for step in STEPS:
            bins_copy(half, step).start()
    for copy in constants + tables_in:
        copy.start()

    for step in STEPS:
        pairs_copy(step).wait()
    own[HALVES].wait()
    lanes = lax.broadcasted_iota(jnp.int32, (ROWS, STATIONS), 1)
    blank = jnp.zeros((8 - 2, ROWS), jnp.int32)
    for block in range(STA):
        rows = jnp.transpose(jnp.concatenate([pairs[block], blank], axis=0))
        hot[block, 0:ROWS] = jnp.where(rows[:, 0:1] == lanes, 1.0, 0.0).astype(BF16)
        second = jnp.where(rows[:, 1:2] == lanes, 1.0, 0.0).astype(BF16)
        for r in range(ROUNDS):
            at = r * PAIRS
            hot[(block + r) % STA, ROWS + at : ROWS + at + PAIRS] = second[at : at + PAIRS]
    for copy in constants:
        copy.wait()

    def pick(half, block):
        re = landing(half, block)[0].astype(F32)
        im = landing(half, block)[1].astype(F32)
        scale = jnp.minimum(lax.rsqrt(re * re + im * im), 4.0)
        for n, part in enumerate((re, im)):
            got = dot(hot[block], (part * scale).astype(BF16))
            u_buf[block, n, :, 0 : CHUNKS[half]] = got[0:ROWS]
            for r in range(ROUNDS):
                at = r * PAIRS
                v_buf[(block - r) % STA, n, at : at + PAIRS, 0 : CHUNKS[half]] = got[ROWS + at : ROWS + at + PAIRS]

    def cross(half, block, taper):
        ur, ui, vr, vi = (buf[block, n, :, 0 : CHUNKS[half]] for buf in (u_buf, v_buf) for n in range(2))
        cr = ((ur * vr + ui * vi) * taper).astype(BF16)
        ci = ((ui * vr - ur * vi) * taper).astype(BF16)
        both = dot(jnp.concatenate([cr, ci], axis=1), forward[2 * STARTS[half] : 2 * (STARTS[half] + CHUNKS[half])])
        y = both[:, 0 : 2 * RANK] + both[:, 2 * RANK :]
        if half > 0:
            y = y + y_sum[block]
        if half < HALVES - 1:
            y_sum[block] = y
        else:
            rows = dot(spread[...], y.astype(BF16)).astype(BF16)
            y_buf[block] = rows.reshape(DAY, SLOT, 2 * RANK)

    def push(block):
        other = lax.rem(s - block + STA, STA)
        for to in range(DAY):
            copy = pltpu.make_async_remote_copy(
                src_ref=y_buf.at[block, to], dst_ref=z_buf.at[me], send_sem=ssem, recv_sem=rsem,
                device_id=(other, to), device_id_type=MESH,
            )
            if block == 0:
                pl.when(to != d)(copy.start)
            else:
                copy.start()

    ramp = 8.0 / BINS
    for half in range(HALVES):
        for step in STEPS:
            bins_copy(half, step).wait()
        own[half].wait()
        for block in range(STA):
            pick(half, block)
        start = s * WIDTH + STARTS[half]
        position = (lax.broadcasted_iota(jnp.int32, (1, CHUNKS[half]), 1) + start).astype(F32) + 0.5
        taper = jnp.minimum(1.0, jnp.minimum(position * ramp, (BINS - position) * ramp))
        order = list(range(STA - 1, -1, -1))
        for n, block in enumerate(order):
            cross(half, block, taper)
            if half == HALVES - 1:
                push(block)
    z_buf[me] = y_buf[0, d]

    for copy in tables_in:
        copy.wait()
    rest = z_buf.at[pl.ds(0, DEVICES - 1)]
    pltpu.make_async_copy(rest, rest, ssem).wait()
    pltpu.make_async_copy(rest, rest, rsem).wait()

    sign = jnp.where(lax.broadcasted_iota(jnp.int32, (1, 2 * RANK), 1) < RANK, 1.0, -1.0)
    for block in range(0, STA, 2):
        rows = [z_buf[n * DAY : (n + 1) * DAY].reshape(DAY * SLOT, 2 * RANK) for n in (block, block + 1)]
        packed = dot(gather[...], jnp.concatenate(rows, axis=1))
        for n in range(2):
            part = packed[:, n * 2 * RANK : (n + 1) * 2 * RANK]
            at = (block + n) * 2 * RANK
            left[0:ROWS, at : at + 2 * RANK] = part.astype(BF16)
            left[ROWS:, at : at + 2 * RANK] = (pltpu.roll(part, RANK, 1) * sign).astype(BF16)
    group = 4 * MINE

    for t in range(TILES):
        both = dot(left[...], table[t])
        re, im = both[0:ROWS], both[ROWS:]
        scale = jnp.minimum(lax.rsqrt(re * re + im * im), 4.0)
        done = []
        for n, part in enumerate((re, re * scale, im * scale)):
            total = part[0:group]
            for g in range(1, ROWS // group):
                total = total + part[g * group : (g + 1) * group]
            sums[t % 2, n] = total
            total = sums[t % 2, n, 0:MINE]
            for g in range(1, 4):
                total = total + sums[t % 2, n, g * MINE : (g + 1) * MINE]
            done.append(total * (1.0 / DAY))
        out_ref[:, t * LAG_TILE : (t + 1) * LAG_TILE] = done[0] * (done[1] * done[1] + done[2] * done[2])


def local(spectra, pair_stations):
    table, forward, spread, gather = (jnp.asarray(a) for a in tables())
    anywhere = pl.BlockSpec(memory_space=pl.ANY)
    dma = pltpu.SemaphoreType.DMA
    return pl.pallas_call(
        correlate,
        name="correlate",
        out_shape=jax.ShapeDtypeStruct((MINE, LAGS), F32),
        in_specs=[anywhere] * 6,
        out_specs=pl.BlockSpec(memory_space=pltpu.VMEM),
        scratch_shapes=[
            pltpu.VMEM((STA, 2, STATIONS, WIDTH), BF16),
            pltpu.VMEM((STA, 2, ROWS), jnp.int32),
            pltpu.VMEM((STA, 2 * ROWS, STATIONS), BF16),
            pltpu.VMEM((STA, 2, ROWS, max(CHUNKS)), F32),
            pltpu.VMEM((STA, 2, ROWS, max(CHUNKS)), F32),
            pltpu.VMEM((STA, ROWS, 2 * RANK), F32),
            pltpu.VMEM((STA, DAY, SLOT, 2 * RANK), BF16),
            pltpu.VMEM((DEVICES, SLOT, 2 * RANK), BF16),
            pltpu.VMEM((2 * ROWS, STA * 2 * RANK), BF16),
            pltpu.VMEM((2, 3, 4 * MINE, LAG_TILE), F32),
            pltpu.VMEM((2 * WIDTH, 4 * RANK), BF16),
            pltpu.VMEM((DAY * SLOT, ROWS), BF16),
            pltpu.VMEM((ROWS, DAY * SLOT), BF16),
            pltpu.VMEM((TILES, STA * 2 * RANK, LAG_TILE), BF16),
            dma((HALVES, STA)),
            dma((HALVES, STA)),
            dma((STA,)),
            dma((STA,)),
            dma((HALVES + 1,)),
            dma((3,)),
            dma((TILES,)),
            dma,
            dma,
        ],
        compiler_params=pltpu.CompilerParams(collective_id=0, has_side_effects=True, vmem_limit_bytes=56 << 20),
    )(spectra.reshape(2, STATIONS, BINS), pair_stations.T, forward, spread, gather, table)


def solution(mesh):
    placed = (P(None, "sta", "day", None), P("sta", None))
    return jax.shard_map(
        local, mesh=mesh, in_specs=placed, out_specs=P(("sta", "day"), None), check_vma=False
    )
```

```python
import functools
import math

import numpy as np
import jax
import jax.numpy as jnp
import ml_dtypes
from jax import lax
from jax.experimental import pallas as pl
from jax.experimental.pallas import tpu as pltpu
from jax.sharding import PartitionSpec as P

BINS = 4096
LAGS = 4096
STA = 8
DAY = 16
STATIONS = 64
ROUNDS = 5
PAIRS = 32
ROWS = ROUNDS * PAIRS
MINE = ROWS // DAY
WIDTH = BINS // STA
RANK = 48
LANES = 64
PIECE = LANES - RANK
GROUP = 4
DEPTH = 2 * (STA // GROUP) * (GROUP - 1) * LANES
SLOT = 16
LAG_TILE = 512
TILES = LAGS // LAG_TILE
CHUNKS = (384, 128)
HALVES = len(CHUNKS)
STARTS = tuple(sum(CHUNKS[:n]) for n in range(HALVES))
DEVICES = STA * DAY
STEPS = range(1, STA)
FIRST_BIN = 36
PERIOD = 72000
MESH = pl.DeviceIdType.MESH
F32 = jnp.float32
BF16 = jnp.bfloat16


def prolate_basis(width, rank):
    t = np.arange(width, dtype=np.float64)
    half_band = LAGS / 2 / PERIOD
    diagonal = ((width - 1 - 2 * t) / 2) ** 2 * np.cos(2 * np.pi * half_band)
    off = t[1:] * (width - t[1:]) / 2
    matrix = np.diag(diagonal) + np.diag(off, 1) + np.diag(off, -1)
    _, vectors = np.linalg.eigh(matrix)
    vectors = vectors[:, ::-1][:, :rank]
    middle = width // 2
    signs = np.sign(vectors[middle])
    return vectors * signs[None]


@functools.lru_cache(maxsize=None)
def tables():
    basis = prolate_basis(WIDTH, RANK)
    lag = np.arange(LAGS, dtype=np.int64) - LAGS // 2
    blocks = []
    for block in range(STA):
        bins = FIRST_BIN + block * WIDTH + np.arange(WIDTH, dtype=np.int64)
        turns = np.remainder(bins[:, None] * lag[None, :], PERIOD)
        angle = turns * (2.0 * np.pi / PERIOD)
        blocks.append((basis.T @ np.cos(angle), -(basis.T @ np.sin(angle))))
    rows = []
    for group in range(0, STA, GROUP):
        for n in range(GROUP - 1):
            for part in range(2):
                rows.append(blocks[group + n][part])
                rows.append(blocks[group + GROUP - 1][part][n * PIECE : (n + 1) * PIECE])
    table = np.concatenate(rows, axis=0) / math.sqrt(BINS)
    table = table.reshape(DEPTH, TILES, LAG_TILE).transpose(1, 0, 2).reshape(TILES * DEPTH, LAG_TILE)
    high = basis.astype(ml_dtypes.bfloat16).astype(np.float64)
    forward = []
    for start, width in zip(STARTS, CHUNKS):
        piece = np.zeros((2, width, 4, LANES))
        for n, part in enumerate((high, basis - high)):
            piece[0, :, 2 * n, 0:RANK] = part[start : start + width]
            piece[1, :, 2 * n + 1, 0:RANK] = part[start : start + width]
        forward.append(piece.reshape(2 * width, 4 * LANES))
    forward = np.concatenate(forward, axis=0)
    spread = np.zeros((DAY * SLOT, ROWS))
    for row in range(ROWS):
        spread[row // MINE * SLOT + row % MINE, row] = 1.0
    spread = np.pad(spread, ((0, 0), (0, DAY * SLOT - ROWS)))
    bank = [table, np.concatenate([forward[:WIDTH], forward[WIDTH:]], axis=1), np.concatenate([spread, spread.T], axis=1)]
    return np.concatenate(bank, axis=0).astype(ml_dtypes.bfloat16)


def dot(a, b):
    return jnp.dot(a, b, preferred_element_type=F32)


def correlate(x_hbm, idx_hbm, bank_hbm, out_ref,
              recv, pairs, hot, u_buf, v_buf, y_sum, y_buf, z_buf, left, sums, forward, spread, gather, table,
              wsem, wrsem, isem, irsem, osem, csem, ssem, rsem):
    s = lax.axis_index("sta")
    d = lax.axis_index("day")
    me = s * DAY + d

    barrier = pltpu.get_barrier_semaphore()
    for step in STEPS:
        pl.semaphore_signal(barrier, inc=1, device_id=(lax.rem(s + step, STA), d), device_id_type=MESH)
    for step in range(1, DAY):
        pl.semaphore_signal(barrier, inc=1, device_id=(s, lax.rem(d + step, DAY)), device_id_type=MESH)

    def bins_of(part, half):
        at = pl.multiple_of(part * WIDTH + STARTS[half], 128)
        return x_hbm.at[:, :, pl.ds(at, CHUNKS[half])]

    def landing(half, block):
        return recv.at[block, :, :, STARTS[half] : STARTS[half] + CHUNKS[half]]

    def bins_copy(half, step):
        to = lax.rem(s + step, STA)
        return pltpu.make_async_remote_copy(
            src_ref=bins_of(to, half), dst_ref=landing(half, step),
            send_sem=wsem.at[half, step], recv_sem=wrsem.at[half, step],
            device_id=(to, d), device_id_type=MESH,
        )

    def pairs_copy(step):
        return pltpu.make_async_remote_copy(
            src_ref=idx_hbm, dst_ref=pairs.at[step], send_sem=isem.at[step], recv_sem=irsem.at[step],
            device_id=(lax.rem(s + step, STA), d), device_id_type=MESH,
        )

    own = [pltpu.make_async_copy(bins_of(s, half), landing(half, 0), osem.at[half]) for half in range(HALVES)]
    own.append(pltpu.make_async_copy(idx_hbm, pairs.at[0], osem.at[HALVES]))
    def bank_copy(row, column, target, n):
        source = bank_hbm.at[row : row + target.shape[0], column : column + target.shape[1]]
        return pltpu.make_async_copy(source, target, csem.at[n])

    side = LAG_TILE // 2
    base = TILES * DEPTH
    tables_in = [bank_copy(t * DEPTH, 0, table.at[t], t) for t in range(TILES)]
    constants = [
        bank_copy(base, 0, forward.at[0:WIDTH], TILES),
        bank_copy(base, side, forward.at[WIDTH : 2 * WIDTH], TILES + 1),
        bank_copy(base + WIDTH, 0, spread, TILES + 2),
        bank_copy(base + WIDTH, side, gather, TILES + 3),
    ]

    for copy in own:
        copy.start()
    pl.semaphore_wait(barrier, STA + DAY - 2)
    for step in STEPS:
        pairs_copy(step).start()
    for half in range(HALVES):
        for step in STEPS:
            bins_copy(half, step).start()
    for copy in constants + tables_in:
        copy.start()

    for step in STEPS:
        pairs_copy(step).wait()
    own[HALVES].wait()
    lanes = lax.broadcasted_iota(jnp.int32, (ROWS, STATIONS), 1)
    blank = jnp.zeros((8 - 2, ROWS), jnp.int32)
    for block in range(STA):
        rows = jnp.transpose(jnp.concatenate([pairs[block], blank], axis=0))
        hot[block, 0:ROWS] = jnp.where(rows[:, 0:1] == lanes, 1.0, 0.0).astype(BF16)
        second = jnp.where(rows[:, 1:2] == lanes, 1.0, 0.0).astype(BF16)
        for r in range(ROUNDS):
            at = r * PAIRS
            hot[(block + r) % STA, ROWS + at : ROWS + at + PAIRS] = second[at : at + PAIRS]
    for copy in constants:
        copy.wait()

    def pick(half, block):
        re = landing(half, block)[0].astype(F32)
        im = landing(half, block)[1].astype(F32)
        scale = jnp.minimum(lax.rsqrt(re * re + im * im), 4.0)
        both = dot(hot[block], jnp.concatenate([re * scale, im * scale], axis=1).astype(BF16))
        for n in range(2):
            got = both[:, n * CHUNKS[half] : (n + 1) * CHUNKS[half]]
            u_buf[block, n, :, 0 : CHUNKS[half]] = got[0:ROWS]
            for r in range(ROUNDS):
                at = r * PAIRS
                v_buf[(block - r) % STA, n, at : at + PAIRS, 0 : CHUNKS[half]] = got[ROWS + at : ROWS + at + PAIRS]

    def cross(half, block, taper):
        ur, ui, vr, vi = (buf[block, n, :, 0 : CHUNKS[half]] for buf in (u_buf, v_buf) for n in range(2))
        cr = ((ur * vr + ui * vi) * taper).astype(BF16)
        ci = ((ui * vr - ur * vi) * taper).astype(BF16)
        both = dot(jnp.concatenate([cr, ci], axis=1), forward[2 * STARTS[half] : 2 * (STARTS[half] + CHUNKS[half])])
        y = both[:, 0 : 2 * LANES] + both[:, 2 * LANES :]
        if half > 0:
            y = y + y_sum[block]
        if half < HALVES - 1:
            y_sum[block] = y
        else:
            rows = dot(spread[:, 0:ROWS], y.astype(BF16)).astype(BF16)
            y_buf[block] = rows.reshape(DAY, SLOT, 2 * LANES)

    def push(block):
        other = lax.rem(s - block + STA, STA)
        for to in range(DAY):
            copy = pltpu.make_async_remote_copy(
                src_ref=y_buf.at[block, to], dst_ref=z_buf.at[me], send_sem=ssem, recv_sem=rsem,
                device_id=(other, to), device_id_type=MESH,
            )
            if block == 0:
                pl.when(to != d)(copy.start)
            else:
                copy.start()

    ramp = 8.0 / BINS
    for half in range(HALVES):
        for step in STEPS:
            bins_copy(half, step).wait()
        own[half].wait()
        for block in range(STA):
            pick(half, block)
        start = s * WIDTH + STARTS[half]
        position = (lax.broadcasted_iota(jnp.int32, (1, CHUNKS[half]), 1) + start).astype(F32) + 0.5
        taper = jnp.minimum(1.0, jnp.minimum(position * ramp, (BINS - position) * ramp))
        order = list(range(STA - 1, -1, -1))
        for n, block in enumerate(order):
            cross(half, block, taper)
            if half == HALVES - 1:
                push(block)
    z_buf[me] = y_buf[0, d]

    for copy in tables_in:
        copy.wait()
    rest = z_buf.at[pl.ds(0, DEVICES - 1)]
    pltpu.make_async_copy(rest, rest, ssem).wait()
    pltpu.make_async_copy(rest, rest, rsem).wait()

    lane = lax.broadcasted_iota(jnp.int32, (1, 2 * LANES), 1)
    sign = jnp.where(lane < LANES, 1.0, -1.0)
    free = lax.rem(lane, LANES) >= RANK
    parts = []
    for block in range(0, STA, 2):
        rows = [z_buf[n * DAY : (n + 1) * DAY].reshape(DAY * SLOT, 2 * LANES) for n in (block, block + 1)]
        packed = dot(gather[0:ROWS], jnp.concatenate(rows, axis=1))
        parts += [packed[:, 0 : 2 * LANES], packed[:, 2 * LANES :]]
    for g in range(0, STA, GROUP):
        for n in range(GROUP - 1):
            part = jnp.where(free, pltpu.roll(parts[g + GROUP - 1], RANK - n * PIECE, 1), parts[g + n])
            at = (g // GROUP * (GROUP - 1) + n) * 2 * LANES
            left[0:ROWS, at : at + 2 * LANES] = part.astype(BF16)
            left[ROWS:, at : at + 2 * LANES] = (pltpu.roll(part, LANES, 1) * sign).astype(BF16)
    group = 4 * MINE

    for t in range(TILES):
        both = dot(left[...], table[t])
        re, im = both[0:ROWS], both[ROWS:]
        scale = jnp.minimum(lax.rsqrt(re * re + im * im), 4.0)
        done = []
        for n, part in enumerate((re, re * scale, im * scale)):
            total = part[0:group]
            for g in range(1, ROWS // group):
                total = total + part[g * group : (g + 1) * group]
            sums[t % 2, n] = total
            total = sums[t % 2, n, 0:MINE]
            for g in range(1, 4):
                total = total + sums[t % 2, n, g * MINE : (g + 1) * MINE]
            done.append(total * (1.0 / DAY))
        out_ref[:, t * LAG_TILE : (t + 1) * LAG_TILE] = done[0] * (done[1] * done[1] + done[2] * done[2])


def local(spectra, pair_stations):
    bank = jnp.asarray(tables())
    anywhere = pl.BlockSpec(memory_space=pl.ANY)
    dma = pltpu.SemaphoreType.DMA
    return pl.pallas_call(
        correlate,
        name="correlate",
        out_shape=jax.ShapeDtypeStruct((MINE, LAGS), F32),
        in_specs=[anywhere] * 3,
        out_specs=pl.BlockSpec(memory_space=pltpu.VMEM),
        scratch_shapes=[
            pltpu.VMEM((STA, 2, STATIONS, WIDTH), BF16),
            pltpu.VMEM((STA, 2, ROWS), jnp.int32),
            pltpu.VMEM((STA, 2 * ROWS, STATIONS), BF16),
            pltpu.VMEM((STA, 2, ROWS, max(CHUNKS)), F32),
            pltpu.VMEM((STA, 2, ROWS, max(CHUNKS)), F32),
            pltpu.VMEM((STA, ROWS, 2 * LANES), F32),
            pltpu.VMEM((STA, DAY, SLOT, 2 * LANES), BF16),
            pltpu.VMEM((DEVICES, SLOT, 2 * LANES), BF16),
            pltpu.VMEM((2 * ROWS, DEPTH), BF16),
            pltpu.VMEM((2, 3, 4 * MINE, LAG_TILE), F32),
            pltpu.VMEM((2 * WIDTH, 4 * LANES), BF16),
            pltpu.VMEM((DAY * SLOT, DAY * SLOT), BF16),
            pltpu.VMEM((DAY * SLOT, DAY * SLOT), BF16),
            pltpu.VMEM((TILES, DEPTH, LAG_TILE), BF16),
            dma((HALVES, STA)),
            dma((HALVES, STA)),
            dma((STA,)),
            dma((STA,)),
            dma((HALVES + 1,)),
            dma((TILES + 4,)),
            dma,
            dma,
        ],
        compiler_params=pltpu.CompilerParams(collective_id=0, has_side_effects=True, vmem_limit_bytes=107 << 19),
    )(spectra.reshape(2, STATIONS, BINS), pair_stations.T, bank)


def solution(mesh):
    placed = (P(None, "sta", "day", None), P("sta", None))
    return jax.shard_map(
        local, mesh=mesh, in_specs=placed, out_specs=P(("sta", "day"), None), check_vma=False
    )
```

```python
import functools
import math

import numpy as np
import jax
import jax.numpy as jnp
import ml_dtypes
from jax import lax
from jax.experimental import pallas as pl
from jax.experimental.pallas import tpu as pltpu
from jax.sharding import PartitionSpec as P

BINS = 4096
LAGS = 4096
STA = 8
DAY = 16
STATIONS = 64
ROUNDS = 5
PAIRS = 32
ROWS = ROUNDS * PAIRS
MINE = ROWS // DAY
WIDTH = BINS // STA
RANK = 48
LANES = 64
PIECE = LANES - RANK
GROUP = 4
DEPTH = 2 * (STA // GROUP) * (GROUP - 1) * LANES
SLOT = 16
LAG_TILE = 512
TILES = LAGS // LAG_TILE
CHUNKS = (384, 128)
HALVES = len(CHUNKS)
STARTS = tuple(sum(CHUNKS[:n]) for n in range(HALVES))
DEVICES = STA * DAY
STEPS = range(1, STA)
FIRST_BIN = 36
PERIOD = 72000
MESH = pl.DeviceIdType.MESH
F32 = jnp.float32
BF16 = jnp.bfloat16


def prolate_basis(width, rank):
    t = np.arange(width, dtype=np.float64)
    half_band = LAGS / 2 / PERIOD
    diagonal = ((width - 1 - 2 * t) / 2) ** 2 * np.cos(2 * np.pi * half_band)
    off = t[1:] * (width - t[1:]) / 2
    matrix = np.diag(diagonal) + np.diag(off, 1) + np.diag(off, -1)
    _, vectors = np.linalg.eigh(matrix)
    vectors = vectors[:, ::-1][:, :rank]
    middle = width // 2
    signs = np.sign(vectors[middle])
    return vectors * signs[None]


@functools.lru_cache(maxsize=None)
def tables():
    basis = prolate_basis(WIDTH, RANK)
    lag = np.arange(LAGS, dtype=np.int64) - LAGS // 2
    blocks = []
    for block in range(STA):
        bins = FIRST_BIN + block * WIDTH + np.arange(WIDTH, dtype=np.int64)
        turns = np.remainder(bins[:, None] * lag[None, :], PERIOD)
        angle = turns * (2.0 * np.pi / PERIOD)
        blocks.append((basis.T @ np.cos(angle), -(basis.T @ np.sin(angle))))
    rows = []
    for group in range(0, STA, GROUP):
        for n in range(GROUP - 1):
            for part in range(2):
                rows.append(blocks[group + n][part])
                rows.append(blocks[group + GROUP - 1][part][n * PIECE : (n + 1) * PIECE])
    table = np.concatenate(rows, axis=0) / math.sqrt(BINS)
    table = table.reshape(DEPTH, TILES, LAG_TILE).transpose(1, 0, 2).reshape(TILES * DEPTH, LAG_TILE)
    high = basis.astype(ml_dtypes.bfloat16).astype(np.float64)
    forward = []
    for start, width in zip(STARTS, CHUNKS):
        piece = np.zeros((2, width, 4, LANES))
        for n, part in enumerate((high, basis - high)):
            piece[0, :, 2 * n, 0:RANK] = part[start : start + width]
            piece[1, :, 2 * n + 1, 0:RANK] = part[start : start + width]
        forward.append(piece.reshape(2 * width, 4 * LANES))
    forward = np.concatenate(forward, axis=0)
    gather = np.zeros((DAY * SLOT, LAG_TILE))
    for row in range(ROWS):
        gather[row, row // MINE * SLOT + row % MINE] = 1.0
    bank = [table, np.concatenate([forward[:WIDTH], forward[WIDTH:]], axis=1), gather]
    return np.concatenate(bank, axis=0).astype(ml_dtypes.bfloat16)


def dot(a, b):
    return jnp.dot(a, b, preferred_element_type=F32)


def correlate(x_hbm, idx_hbm, bank_hbm, out_ref,
              recv, pairs, hot, u_buf, v_buf, y_sum, y_buf, z_buf, left, sums, forward, gather, table,
              wsem, wrsem, isem, irsem, osem, csem, ssem, rsem):
    s = lax.axis_index("sta")
    d = lax.axis_index("day")
    me = s * DAY + d

    barrier = pltpu.get_barrier_semaphore()
    for step in STEPS:
        pl.semaphore_signal(barrier, inc=1, device_id=(lax.rem(s + step, STA), d), device_id_type=MESH)
    for step in range(1, DAY):
        pl.semaphore_signal(barrier, inc=1, device_id=(s, lax.rem(d + step, DAY)), device_id_type=MESH)

    def bins_of(part, half):
        at = pl.multiple_of(part * WIDTH + STARTS[half], 128)
        return x_hbm.at[:, :, pl.ds(at, CHUNKS[half])]

    def landing(half, block):
        return recv.at[block, :, :, STARTS[half] : STARTS[half] + CHUNKS[half]]

    def bins_copy(half, step):
        to = lax.rem(s + step, STA)
        return pltpu.make_async_remote_copy(
            src_ref=bins_of(to, half), dst_ref=landing(half, step),
            send_sem=wsem.at[half, step], recv_sem=wrsem.at[half, step],
            device_id=(to, d), device_id_type=MESH,
        )

    def pairs_copy(step):
        return pltpu.make_async_remote_copy(
            src_ref=idx_hbm, dst_ref=pairs.at[step], send_sem=isem.at[step], recv_sem=irsem.at[step],
            device_id=(lax.rem(s + step, STA), d), device_id_type=MESH,
        )

    own = [pltpu.make_async_copy(bins_of(s, half), landing(half, 0), osem.at[half]) for half in range(HALVES)]
    own.append(pltpu.make_async_copy(idx_hbm, pairs.at[0], osem.at[HALVES]))
    def bank_copy(row, column, target, n):
        source = bank_hbm.at[row : row + target.shape[0], column : column + target.shape[1]]
        return pltpu.make_async_copy(source, target, csem.at[n])

    side = LAG_TILE // 2
    base = TILES * DEPTH
    tables_in = [bank_copy(t * DEPTH, 0, table.at[t], t) for t in range(TILES)]
    constants = [
        bank_copy(base, 0, forward.at[0:WIDTH], TILES),
        bank_copy(base, side, forward.at[WIDTH : 2 * WIDTH], TILES + 1),
        bank_copy(base + WIDTH, 0, gather, TILES + 2),
    ]

    for copy in own:
        copy.start()
    pl.semaphore_wait(barrier, STA + DAY - 2)
    for step in STEPS:
        pairs_copy(step).start()
    for half in range(HALVES):
        for step in STEPS:
            bins_copy(half, step).start()
    for copy in constants + tables_in:
        copy.start()

    for step in STEPS:
        pairs_copy(step).wait()
    own[HALVES].wait()
    y_sum[:, ROWS:, :] = jnp.zeros((STA, SLOT, 2 * LANES), F32)
    lanes = lax.broadcasted_iota(jnp.int32, (ROWS, STATIONS), 1)
    blank = jnp.zeros((8 - 2, ROWS), jnp.int32)
    for block in range(STA):
        rows = jnp.transpose(jnp.concatenate([pairs[block], blank], axis=0))
        hot[block, 0:ROWS] = jnp.where(rows[:, 0:1] == lanes, 1.0, 0.0).astype(BF16)
        second = jnp.where(rows[:, 1:2] == lanes, 1.0, 0.0).astype(BF16)
        for r in range(ROUNDS):
            at = r * PAIRS
            hot[(block + r) % STA, ROWS + at : ROWS + at + PAIRS] = second[at : at + PAIRS]
    for copy in constants:
        copy.wait()

    def pick(half, block):
        re = landing(half, block)[0].astype(F32)
        im = landing(half, block)[1].astype(F32)
        scale = jnp.minimum(lax.rsqrt(re * re + im * im), 4.0)
        both = dot(hot[block], jnp.concatenate([re * scale, im * scale], axis=1).astype(BF16))
        for n in range(2):
            got = both[:, n * CHUNKS[half] : (n + 1) * CHUNKS[half]]
            u_buf[block, n, :, 0 : CHUNKS[half]] = got[0:ROWS]
            for r in range(ROUNDS):
                at = r * PAIRS
                v_buf[(block - r) % STA, n, at : at + PAIRS, 0 : CHUNKS[half]] = got[ROWS + at : ROWS + at + PAIRS]

    def cross(half, block, taper):
        ur, ui, vr, vi = (buf[block, n, :, 0 : CHUNKS[half]] for buf in (u_buf, v_buf) for n in range(2))
        cr = ((ur * vr + ui * vi) * taper).astype(BF16)
        ci = ((ui * vr - ur * vi) * taper).astype(BF16)
        both = dot(jnp.concatenate([cr, ci], axis=1), forward[2 * STARTS[half] : 2 * (STARTS[half] + CHUNKS[half])])
        y = both[:, 0 : 2 * LANES] + both[:, 2 * LANES :]
        if half > 0:
            y = y + y_sum[block, 0:ROWS]
        if half < HALVES - 1:
            y_sum[block, 0:ROWS] = y
        else:
            y_sum[block, 0:ROWS] = y
            for to in range(DAY):
                y_buf[block, to] = y_sum[block, to * MINE : to * MINE + SLOT].astype(BF16)

    def push(block):
        other = lax.rem(s - block + STA, STA)
        for to in range(DAY):
            copy = pltpu.make_async_remote_copy(
                src_ref=y_buf.at[block, to], dst_ref=z_buf.at[me], send_sem=ssem, recv_sem=rsem,
                device_id=(other, to), device_id_type=MESH,
            )
            if block == 0:
                pl.when(to != d)(copy.start)
            else:
                copy.start()

    ramp = 8.0 / BINS
    for half in range(HALVES):
        for step in STEPS:
            bins_copy(half, step).wait()
        own[half].wait()
        for block in range(STA):
            pick(half, block)
        start = s * WIDTH + STARTS[half]
        position = (lax.broadcasted_iota(jnp.int32, (1, CHUNKS[half]), 1) + start).astype(F32) + 0.5
        taper = jnp.minimum(1.0, jnp.minimum(position * ramp, (BINS - position) * ramp))
        order = list(range(STA - 1, -1, -1))
        for n, block in enumerate(order):
            cross(half, block, taper)
            if half == HALVES - 1 and n > 0:
                push(order[n - 1])
    push(order[-1])
    z_buf[me] = y_buf[0, d]

    for copy in tables_in:
        copy.wait()
    rest = z_buf.at[pl.ds(0, DEVICES - 1)]
    pltpu.make_async_copy(rest, rest, rsem).wait()

    lane = lax.broadcasted_iota(jnp.int32, (1, 2 * LANES), 1)
    sign = jnp.where(lane < LANES, 1.0, -1.0)
    free = lax.rem(lane, LANES) >= RANK
    parts = []
    for block in range(0, STA, 2):
        rows = [z_buf[n * DAY : (n + 1) * DAY].reshape(DAY * SLOT, 2 * LANES) for n in (block, block + 1)]
        packed = dot(gather[0:ROWS], jnp.concatenate(rows, axis=1))
        parts += [packed[:, 0 : 2 * LANES], packed[:, 2 * LANES :]]
    for g in range(0, STA, GROUP):
        for n in range(GROUP - 1):
            part = jnp.where(free, pltpu.roll(parts[g + GROUP - 1], RANK - n * PIECE, 1), parts[g + n])
            at = (g // GROUP * (GROUP - 1) + n) * 2 * LANES
            left[0:ROWS, at : at + 2 * LANES] = part.astype(BF16)
            left[ROWS:, at : at + 2 * LANES] = (pltpu.roll(part, LANES, 1) * sign).astype(BF16)
    group = 4 * MINE

    for t in range(TILES):
        both = dot(left[...], table[t])
        re, im = both[0:ROWS], both[ROWS:]
        scale = jnp.minimum(lax.rsqrt(re * re + im * im), 4.0)
        done = []
        for n, part in enumerate((re, re * scale, im * scale)):
            total = part[0:group]
            for g in range(1, ROWS // group):
                total = total + part[g * group : (g + 1) * group]
            sums[t % 2, n] = total
            total = sums[t % 2, n, 0:MINE]
            for g in range(1, 4):
                total = total + sums[t % 2, n, g * MINE : (g + 1) * MINE]
            done.append(total * (1.0 / DAY))
        out_ref[:, t * LAG_TILE : (t + 1) * LAG_TILE] = done[0] * (done[1] * done[1] + done[2] * done[2])
    pltpu.make_async_copy(rest, rest, ssem).wait()


def local(spectra, pair_stations):
    bank = jnp.asarray(tables())
    anywhere = pl.BlockSpec(memory_space=pl.ANY)
    dma = pltpu.SemaphoreType.DMA
    return pl.pallas_call(
        correlate,
        name="correlate",
        out_shape=jax.ShapeDtypeStruct((MINE, LAGS), F32),
        in_specs=[anywhere] * 3,
        out_specs=pl.BlockSpec(memory_space=pltpu.VMEM),
        scratch_shapes=[
            pltpu.VMEM((STA, 2, STATIONS, WIDTH), BF16),
            pltpu.VMEM((STA, 2, ROWS), jnp.int32),
            pltpu.VMEM((STA, 2 * ROWS, STATIONS), BF16),
            pltpu.VMEM((STA, 2, ROWS, max(CHUNKS)), F32),
            pltpu.VMEM((STA, 2, ROWS, max(CHUNKS)), F32),
            pltpu.VMEM((STA, ROWS + SLOT, 2 * LANES), F32),
            pltpu.VMEM((STA, DAY, SLOT, 2 * LANES), BF16),
            pltpu.VMEM((DEVICES, SLOT, 2 * LANES), BF16),
            pltpu.VMEM((2 * ROWS, DEPTH), BF16),
            pltpu.VMEM((2, 3, 4 * MINE, LAG_TILE), F32),
            pltpu.VMEM((2 * WIDTH, 4 * LANES), BF16),
            pltpu.VMEM((DAY * SLOT, DAY * SLOT), BF16),
            pltpu.VMEM((TILES, DEPTH, LAG_TILE), BF16),
            dma((HALVES, STA)),
            dma((HALVES, STA)),
            dma((STA,)),
            dma((STA,)),
            dma((HALVES + 1,)),
            dma((TILES + 3,)),
            dma,
            dma,
        ],
        compiler_params=pltpu.CompilerParams(collective_id=0, has_side_effects=True, vmem_limit_bytes=107 << 19),
    )(spectra.reshape(2, STATIONS, BINS), pair_stations.T, bank)


def solution(mesh):
    placed = (P(None, "sta", "day", None), P("sta", None))
    return jax.shard_map(
        local, mesh=mesh, in_specs=placed, out_specs=P(("sta", "day"), None), check_vma=False
    )
```

```python
import functools
import math

import numpy as np
import jax
import jax.numpy as jnp
import ml_dtypes
from jax import lax
from jax.experimental import pallas as pl
from jax.experimental.pallas import tpu as pltpu
from jax.sharding import PartitionSpec as P

BINS = 4096
LAGS = 4096
STA = 8
DAY = 16
STATIONS = 64
ROUNDS = 5
PAIRS = 32
ROWS = ROUNDS * PAIRS
MINE = ROWS // DAY
WIDTH = BINS // STA
RANK = 48
LANES = 64
PIECE = LANES - RANK
GROUP = 4
DEPTH = 2 * (STA // GROUP) * (GROUP - 1) * LANES
SLOT = 16
LAG_TILE = 512
TILES = LAGS // LAG_TILE
CHUNKS = (384, 128)
HALVES = len(CHUNKS)
STARTS = tuple(sum(CHUNKS[:n]) for n in range(HALVES))
DEVICES = STA * DAY
STEPS = range(1, STA)
FIRST_BIN = 36
PERIOD = 72000
MESH = pl.DeviceIdType.MESH
F32 = jnp.float32
BF16 = jnp.bfloat16


def prolate_basis(width, rank):
    t = np.arange(width, dtype=np.float64)
    half_band = LAGS / 2 / PERIOD
    diagonal = ((width - 1 - 2 * t) / 2) ** 2 * np.cos(2 * np.pi * half_band)
    off = t[1:] * (width - t[1:]) / 2
    matrix = np.diag(diagonal) + np.diag(off, 1) + np.diag(off, -1)
    _, vectors = np.linalg.eigh(matrix)
    vectors = vectors[:, ::-1][:, :rank]
    middle = width // 2
    signs = np.sign(vectors[middle])
    return vectors * signs[None]


@functools.lru_cache(maxsize=None)
def tables():
    basis = prolate_basis(WIDTH, RANK)
    lag = np.arange(LAGS, dtype=np.int64) - LAGS // 2
    blocks = []
    for block in range(STA):
        bins = FIRST_BIN + block * WIDTH + np.arange(WIDTH, dtype=np.int64)
        turns = np.remainder(bins[:, None] * lag[None, :], PERIOD)
        angle = turns * (2.0 * np.pi / PERIOD)
        blocks.append((basis.T @ np.cos(angle), -(basis.T @ np.sin(angle))))
    rows = []
    for group in range(0, STA, GROUP):
        for n in range(GROUP - 1):
            for part in range(2):
                rows.append(blocks[group + n][part])
                rows.append(blocks[group + GROUP - 1][part][n * PIECE : (n + 1) * PIECE])
    table = np.concatenate(rows, axis=0) / math.sqrt(BINS)
    table = table.reshape(DEPTH, TILES, LAG_TILE).transpose(1, 0, 2).reshape(TILES * DEPTH, LAG_TILE)
    high = basis.astype(ml_dtypes.bfloat16).astype(np.float64)
    forward = []
    for start, width in zip(STARTS, CHUNKS):
        piece = np.zeros((2, width, 4, LANES))
        for n, part in enumerate((high, basis - high)):
            piece[0, :, 2 * n, 0:RANK] = part[start : start + width]
            piece[1, :, 2 * n + 1, 0:RANK] = part[start : start + width]
        forward.append(piece.reshape(2 * width, 4 * LANES))
    forward = np.concatenate(forward, axis=0)
    bank = [table, np.concatenate([forward[:WIDTH], forward[WIDTH:]], axis=1)]
    return np.concatenate(bank, axis=0).astype(ml_dtypes.bfloat16)


def dot(a, b):
    return jnp.dot(a, b, preferred_element_type=F32)


def correlate(x_hbm, idx_hbm, bank_hbm, out_ref,
              recv, pairs, hot, u_buf, v_buf, y_sum, y_buf, z_buf, left, sums, forward, table,
              wsem, wrsem, isem, irsem, osem, csem, ssem, rsem):
    s = lax.axis_index("sta")
    d = lax.axis_index("day")
    me = s * DAY + d

    barrier = pltpu.get_barrier_semaphore()
    for step in STEPS:
        pl.semaphore_signal(barrier, inc=1, device_id=(lax.rem(s + step, STA), d), device_id_type=MESH)
    for step in range(1, DAY):
        pl.semaphore_signal(barrier, inc=1, device_id=(s, lax.rem(d + step, DAY)), device_id_type=MESH)

    def bins_of(part, half):
        at = pl.multiple_of(part * WIDTH + STARTS[half], 128)
        return x_hbm.at[:, :, pl.ds(at, CHUNKS[half])]

    def landing(half, block):
        return recv.at[block, :, :, STARTS[half] : STARTS[half] + CHUNKS[half]]

    def bins_copy(half, step):
        to = lax.rem(s + step, STA)
        return pltpu.make_async_remote_copy(
            src_ref=bins_of(to, half), dst_ref=landing(half, step),
            send_sem=wsem.at[half, step], recv_sem=wrsem.at[half, step],
            device_id=(to, d), device_id_type=MESH,
        )

    def pairs_copy(step):
        return pltpu.make_async_remote_copy(
            src_ref=idx_hbm, dst_ref=pairs.at[step], send_sem=isem.at[step], recv_sem=irsem.at[step],
            device_id=(lax.rem(s + step, STA), d), device_id_type=MESH,
        )

    own = [pltpu.make_async_copy(bins_of(s, half), landing(half, 0), osem.at[half]) for half in range(HALVES)]
    own.append(pltpu.make_async_copy(idx_hbm, pairs.at[0], osem.at[HALVES]))
    def bank_copy(row, column, target, n):
        source = bank_hbm.at[row : row + target.shape[0], column : column + target.shape[1]]
        return pltpu.make_async_copy(source, target, csem.at[n])

    side = LAG_TILE // 2
    base = TILES * DEPTH
    tables_in = [bank_copy(t * DEPTH, 0, table.at[t], t) for t in range(TILES)]
    constants = [
        bank_copy(base, 0, forward.at[0:WIDTH], TILES),
        bank_copy(base, side, forward.at[WIDTH : 2 * WIDTH], TILES + 1),
    ]

    for copy in own:
        copy.start()
    pl.semaphore_wait(barrier, STA + DAY - 2)
    for step in STEPS:
        pairs_copy(step).start()
    for half in range(HALVES):
        for step in STEPS:
            bins_copy(half, step).start()
    for copy in constants + tables_in:
        copy.start()

    for step in STEPS:
        pairs_copy(step).wait()
    own[HALVES].wait()
    y_sum[:, ROWS:, :] = jnp.zeros((STA, SLOT, 2 * LANES), F32)
    lanes = lax.broadcasted_iota(jnp.int32, (ROWS, STATIONS), 1)
    blank = jnp.zeros((8 - 2, ROWS), jnp.int32)
    for block in range(STA):
        rows = jnp.transpose(jnp.concatenate([pairs[block], blank], axis=0))
        hot[block, 0:ROWS] = jnp.where(rows[:, 0:1] == lanes, 1.0, 0.0).astype(BF16)
        second = jnp.where(rows[:, 1:2] == lanes, 1.0, 0.0).astype(BF16)
        for r in range(ROUNDS):
            at = r * PAIRS
            hot[(block + r) % STA, ROWS + at : ROWS + at + PAIRS] = second[at : at + PAIRS]
    for copy in constants:
        copy.wait()

    def pick(half, block):
        re = landing(half, block)[0].astype(F32)
        im = landing(half, block)[1].astype(F32)
        scale = jnp.minimum(lax.rsqrt(re * re + im * im), 4.0)
        both = dot(hot[block], jnp.concatenate([re * scale, im * scale], axis=1).astype(BF16))
        for n in range(2):
            got = both[:, n * CHUNKS[half] : (n + 1) * CHUNKS[half]]
            u_buf[block, n, :, 0 : CHUNKS[half]] = got[0:ROWS]
            for r in range(ROUNDS):
                at = r * PAIRS
                v_buf[(block - r) % STA, n, at : at + PAIRS, 0 : CHUNKS[half]] = got[ROWS + at : ROWS + at + PAIRS]

    def cross(half, block, taper):
        ur, ui, vr, vi = (buf[block, n, :, 0 : CHUNKS[half]] for buf in (u_buf, v_buf) for n in range(2))
        cr = ((ur * vr + ui * vi) * taper).astype(BF16)
        ci = ((ui * vr - ur * vi) * taper).astype(BF16)
        both = dot(jnp.concatenate([cr, ci], axis=1), forward[2 * STARTS[half] : 2 * (STARTS[half] + CHUNKS[half])])
        y = both[:, 0 : 2 * LANES] + both[:, 2 * LANES :]
        if half > 0:
            y = y + y_sum[block, 0:ROWS]
        if half < HALVES - 1:
            y_sum[block, 0:ROWS] = y
        else:
            y_sum[block, 0:ROWS] = y
            for to in range(DAY):
                y_buf[block, to] = y_sum[block, to * MINE : to * MINE + SLOT].astype(BF16)

    def push(block):
        other = lax.rem(s - block + STA, STA)
        for to in range(DAY):
            copy = pltpu.make_async_remote_copy(
                src_ref=y_buf.at[block, to], dst_ref=z_buf.at[me], send_sem=ssem, recv_sem=rsem,
                device_id=(other, to), device_id_type=MESH,
            )
            if block == 0:
                pl.when(to != d)(copy.start)
            else:
                copy.start()

    ramp = 8.0 / BINS
    for half in range(HALVES):
        for step in STEPS:
            bins_copy(half, step).wait()
        own[half].wait()
        for block in range(STA):
            pick(half, block)
        start = s * WIDTH + STARTS[half]
        position = (lax.broadcasted_iota(jnp.int32, (1, CHUNKS[half]), 1) + start).astype(F32) + 0.5
        taper = jnp.minimum(1.0, jnp.minimum(position * ramp, (BINS - position) * ramp))
        order = list(range(STA - 1, -1, -1))
        for n, block in enumerate(order):
            cross(half, block, taper)
            if half == HALVES - 1 and n > 0:
                push(order[n - 1])
    push(order[-1])
    z_buf[me] = y_buf[0, d]

    for copy in tables_in:
        copy.wait()
    rest = z_buf.at[pl.ds(0, DEVICES - 1)]
    pltpu.make_async_copy(rest, rest, rsem).wait()

    lane = lax.broadcasted_iota(jnp.int32, (1, 2 * LANES), 1)
    sign = jnp.where(lane < LANES, 1.0, -1.0)
    free = lax.rem(lane, LANES) >= RANK
    parts = []
    for block in range(STA):
        for day in range(DAY):
            y_sum[block, day * MINE : day * MINE + SLOT] = z_buf[block * DAY + day].astype(F32)
        parts.append(y_sum[block, 0:ROWS])
    for g in range(0, STA, GROUP):
        for n in range(GROUP - 1):
            part = jnp.where(free, pltpu.roll(parts[g + GROUP - 1], RANK - n * PIECE, 1), parts[g + n])
            at = (g // GROUP * (GROUP - 1) + n) * 2 * LANES
            left[0:ROWS, at : at + 2 * LANES] = part.astype(BF16)
            left[ROWS:, at : at + 2 * LANES] = (pltpu.roll(part, LANES, 1) * sign).astype(BF16)
    group = 4 * MINE

    for t in range(TILES):
        both = dot(left[...], table[t])
        re, im = both[0:ROWS], both[ROWS:]
        scale = jnp.minimum(lax.rsqrt(re * re + im * im), 4.0)
        done = []
        for n, part in enumerate((re, re * scale, im * scale)):
            total = part[0:group]
            for g in range(1, ROWS // group):
                total = total + part[g * group : (g + 1) * group]
            sums[t % 2, n] = total
            total = sums[t % 2, n, 0:MINE]
            for g in range(1, 4):
                total = total + sums[t % 2, n, g * MINE : (g + 1) * MINE]
            done.append(total * (1.0 / DAY))
        out_ref[:, t * LAG_TILE : (t + 1) * LAG_TILE] = done[0] * (done[1] * done[1] + done[2] * done[2])
    pltpu.make_async_copy(rest, rest, ssem).wait()


def local(spectra, pair_stations):
    bank = jnp.asarray(tables())
    anywhere = pl.BlockSpec(memory_space=pl.ANY)
    dma = pltpu.SemaphoreType.DMA
    return pl.pallas_call(
        correlate,
        name="correlate",
        out_shape=jax.ShapeDtypeStruct((MINE, LAGS), F32),
        in_specs=[anywhere] * 3,
        out_specs=pl.BlockSpec(memory_space=pltpu.VMEM),
        scratch_shapes=[
            pltpu.VMEM((STA, 2, STATIONS, WIDTH), BF16),
            pltpu.VMEM((STA, 2, ROWS), jnp.int32),
            pltpu.VMEM((STA, 2 * ROWS, STATIONS), BF16),
            pltpu.VMEM((STA, 2, ROWS, max(CHUNKS)), F32),
            pltpu.VMEM((STA, 2, ROWS, max(CHUNKS)), F32),
            pltpu.VMEM((STA, ROWS + SLOT, 2 * LANES), F32),
            pltpu.VMEM((STA, DAY, SLOT, 2 * LANES), BF16),
            pltpu.VMEM((DEVICES, SLOT, 2 * LANES), BF16),
            pltpu.VMEM((2 * ROWS, DEPTH), BF16),
            pltpu.VMEM((2, 3, 4 * MINE, LAG_TILE), F32),
            pltpu.VMEM((2 * WIDTH, 4 * LANES), BF16),
            pltpu.VMEM((TILES, DEPTH, LAG_TILE), BF16),
            dma((HALVES, STA)),
            dma((HALVES, STA)),
            dma((STA,)),
            dma((STA,)),
            dma((HALVES + 1,)),
            dma((TILES + 2,)),
            dma,
            dma,
        ],
        compiler_params=pltpu.CompilerParams(collective_id=0, has_side_effects=True, vmem_limit_bytes=107 << 19),
    )(spectra.reshape(2, STATIONS, BINS), pair_stations.T, bank)


def solution(mesh):
    placed = (P(None, "sta", "day", None), P("sta", None))
    return jax.shard_map(
        local, mesh=mesh, in_specs=placed, out_specs=P(("sta", "day"), None), check_vma=False
    )
```

```python
import functools
import math

import numpy as np
import jax
import jax.numpy as jnp
import ml_dtypes
from jax import lax
from jax.experimental import pallas as pl
from jax.experimental.pallas import tpu as pltpu
from jax.sharding import PartitionSpec as P

BINS = 4096
LAGS = 4096
STA = 8
DAY = 16
STATIONS = 64
ROUNDS = 5
PAIRS = 32
ROWS = ROUNDS * PAIRS
MINE = ROWS // DAY
WIDTH = BINS // STA
RANK = 48
LANES = 64
PIECE = LANES - RANK
GROUP = 4
DEPTH = 2 * (STA // GROUP) * (GROUP - 1) * LANES
SLOT = 16
LAG_TILE = 512
TILES = LAGS // LAG_TILE
CHUNKS = (256, 128, 128)
HALVES = len(CHUNKS)
STARTS = tuple(sum(CHUNKS[:n]) for n in range(HALVES))
DEVICES = STA * DAY
STEPS = range(1, STA)
FIRST_BIN = 36
PERIOD = 72000
MESH = pl.DeviceIdType.MESH
F32 = jnp.float32
BF16 = jnp.bfloat16


def prolate_basis(width, rank):
    t = np.arange(width, dtype=np.float64)
    half_band = LAGS / 2 / PERIOD
    diagonal = ((width - 1 - 2 * t) / 2) ** 2 * np.cos(2 * np.pi * half_band)
    off = t[1:] * (width - t[1:]) / 2
    matrix = np.diag(diagonal) + np.diag(off, 1) + np.diag(off, -1)
    _, vectors = np.linalg.eigh(matrix)
    vectors = vectors[:, ::-1][:, :rank]
    middle = width // 2
    signs = np.sign(vectors[middle])
    return vectors * signs[None]


@functools.lru_cache(maxsize=None)
def tables():
    basis = prolate_basis(WIDTH, RANK)
    lag = np.arange(LAGS, dtype=np.int64) - LAGS // 2
    blocks = []
    for block in range(STA):
        bins = FIRST_BIN + block * WIDTH + np.arange(WIDTH, dtype=np.int64)
        turns = np.remainder(bins[:, None] * lag[None, :], PERIOD)
        angle = turns * (2.0 * np.pi / PERIOD)
        blocks.append((basis.T @ np.cos(angle), -(basis.T @ np.sin(angle))))
    rows = []
    for group in range(0, STA, GROUP):
        for n in range(GROUP - 1):
            for part in range(2):
                rows.append(blocks[group + n][part])
                rows.append(blocks[group + GROUP - 1][part][n * PIECE : (n + 1) * PIECE])
    table = np.concatenate(rows, axis=0) / math.sqrt(BINS)
    table = table.reshape(DEPTH, TILES, LAG_TILE).transpose(1, 0, 2).reshape(TILES * DEPTH, LAG_TILE)
    high = basis.astype(ml_dtypes.bfloat16).astype(np.float64)
    forward = []
    for start, width in zip(STARTS, CHUNKS):
        piece = np.zeros((2, width, 4, LANES))
        for n, part in enumerate((high, basis - high)):
            piece[0, :, 2 * n, 0:RANK] = part[start : start + width]
            piece[1, :, 2 * n + 1, 0:RANK] = part[start : start + width]
        forward.append(piece.reshape(2 * width, 4 * LANES))
    forward = np.concatenate(forward, axis=0)
    gather = np.zeros((DAY * SLOT, LAG_TILE))
    for row in range(ROWS):
        gather[row, row // MINE * SLOT + row % MINE] = 1.0
    bank = [table, np.concatenate([forward[:WIDTH], forward[WIDTH:]], axis=1), gather]
    return np.concatenate(bank, axis=0).astype(ml_dtypes.bfloat16)


def dot(a, b):
    return jnp.dot(a, b, preferred_element_type=F32)


def correlate(x_hbm, idx_hbm, bank_hbm, out_ref,
              recv, pairs, hot, u_buf, v_buf, y_sum, y_buf, z_buf, left, sums, forward, gather, table,
              wsem, wrsem, isem, irsem, osem, csem, ssem, rsem):
    s = lax.axis_index("sta")
    d = lax.axis_index("day")
    me = s * DAY + d

    barrier = pltpu.get_barrier_semaphore()
    for step in STEPS:
        pl.semaphore_signal(barrier, inc=1, device_id=(lax.rem(s + step, STA), d), device_id_type=MESH)
    for step in range(1, DAY):
        pl.semaphore_signal(barrier, inc=1, device_id=(s, lax.rem(d + step, DAY)), device_id_type=MESH)

    def bins_of(part, half):
        at = pl.multiple_of(part * WIDTH + STARTS[half], 128)
        return x_hbm.at[:, :, pl.ds(at, CHUNKS[half])]

    def landing(half, block):
        return recv.at[block, :, :, STARTS[half] : STARTS[half] + CHUNKS[half]]

    def bins_copy(half, step):
        to = lax.rem(s + step, STA)
        return pltpu.make_async_remote_copy(
            src_ref=bins_of(to, half), dst_ref=landing(half, step),
            send_sem=wsem.at[half, step], recv_sem=wrsem.at[half, step],
            device_id=(to, d), device_id_type=MESH,
        )

    def pairs_copy(step):
        return pltpu.make_async_remote_copy(
            src_ref=idx_hbm, dst_ref=pairs.at[step], send_sem=isem.at[step], recv_sem=irsem.at[step],
            device_id=(lax.rem(s + step, STA), d), device_id_type=MESH,
        )

    own = [pltpu.make_async_copy(bins_of(s, half), landing(half, 0), osem.at[half]) for half in range(HALVES)]
    own.append(pltpu.make_async_copy(idx_hbm, pairs.at[0], osem.at[HALVES]))
    def bank_copy(row, column, target, n):
        source = bank_hbm.at[row : row + target.shape[0], column : column + target.shape[1]]
        return pltpu.make_async_copy(source, target, csem.at[n])

    side = LAG_TILE // 2
    base = TILES * DEPTH
    tables_in = [bank_copy(t * DEPTH, 0, table.at[t], t) for t in range(TILES)]
    constants = [
        bank_copy(base, 0, forward.at[0:WIDTH], TILES),
        bank_copy(base, side, forward.at[WIDTH : 2 * WIDTH], TILES + 1),
        bank_copy(base + WIDTH, 0, gather, TILES + 2),
    ]

    for copy in own:
        copy.start()
    pl.semaphore_wait(barrier, STA + DAY - 2)
    for step in STEPS:
        pairs_copy(step).start()
    for half in range(HALVES):
        for step in STEPS:
            bins_copy(half, step).start()
    for copy in constants + tables_in:
        copy.start()

    for step in STEPS:
        pairs_copy(step).wait()
    own[HALVES].wait()
    y_sum[:, ROWS:, :] = jnp.zeros((STA, SLOT, 2 * LANES), F32)
    lanes = lax.broadcasted_iota(jnp.int32, (ROWS, STATIONS), 1)
    blank = jnp.zeros((8 - 2, ROWS), jnp.int32)
    for block in range(STA):
        rows = jnp.transpose(jnp.concatenate([pairs[block], blank], axis=0))
        hot[block, 0:ROWS] = jnp.where(rows[:, 0:1] == lanes, 1.0, 0.0).astype(BF16)
        second = jnp.where(rows[:, 1:2] == lanes, 1.0, 0.0).astype(BF16)
        for r in range(ROUNDS):
            at = r * PAIRS
            hot[(block + r) % STA, ROWS + at : ROWS + at + PAIRS] = second[at : at + PAIRS]
    for copy in constants:
        copy.wait()

    def pick(half, block):
        re = landing(half, block)[0].astype(F32)
        im = landing(half, block)[1].astype(F32)
        scale = jnp.minimum(lax.rsqrt(re * re + im * im), 4.0)
        both = dot(hot[block], jnp.concatenate([re * scale, im * scale], axis=1).astype(BF16))
        for n in range(2):
            got = both[:, n * CHUNKS[half] : (n + 1) * CHUNKS[half]]
            u_buf[block, n, :, 0 : CHUNKS[half]] = got[0:ROWS]
            for r in range(ROUNDS):
                at = r * PAIRS
                v_buf[(block - r) % STA, n, at : at + PAIRS, 0 : CHUNKS[half]] = got[ROWS + at : ROWS + at + PAIRS]

    def cross(half, block, taper):
        ur, ui, vr, vi = (buf[block, n, :, 0 : CHUNKS[half]] for buf in (u_buf, v_buf) for n in range(2))
        cr = ((ur * vr + ui * vi) * taper).astype(BF16)
        ci = ((ui * vr - ur * vi) * taper).astype(BF16)
        both = dot(jnp.concatenate([cr, ci], axis=1), forward[2 * STARTS[half] : 2 * (STARTS[half] + CHUNKS[half])])
        y = both[:, 0 : 2 * LANES] + both[:, 2 * LANES :]
        if half > 0:
            y = y + y_sum[block, 0:ROWS]
        if half < HALVES - 1:
            y_sum[block, 0:ROWS] = y
        else:
            y_sum[block, 0:ROWS] = y
            for to in range(DAY):
                y_buf[block, to] = y_sum[block, to * MINE : to * MINE + SLOT].astype(BF16)

    def push(block):
        other = lax.rem(s - block + STA, STA)
        for to in range(DAY):
            copy = pltpu.make_async_remote_copy(
                src_ref=y_buf.at[block, to], dst_ref=z_buf.at[me], send_sem=ssem, recv_sem=rsem,
                device_id=(other, to), device_id_type=MESH,
            )
            if block == 0:
                pl.when(to != d)(copy.start)
            else:
                copy.start()

    ramp = 8.0 / BINS
    for half in range(HALVES):
        for step in STEPS:
            bins_copy(half, step).wait()
        own[half].wait()
        for block in range(STA):
            pick(half, block)
        start = s * WIDTH + STARTS[half]
        position = (lax.broadcasted_iota(jnp.int32, (1, CHUNKS[half]), 1) + start).astype(F32) + 0.5
        taper = jnp.minimum(1.0, jnp.minimum(position * ramp, (BINS - position) * ramp))
        order = list(range(STA - 1, -1, -1))
        for n, block in enumerate(order):
            cross(half, block, taper)
            if half == HALVES - 1 and n > 0:
                push(order[n - 1])
    push(order[-1])
    z_buf[me] = y_buf[0, d]

    for copy in tables_in:
        copy.wait()
    rest = z_buf.at[pl.ds(0, DEVICES - 1)]
    pltpu.make_async_copy(rest, rest, rsem).wait()

    lane = lax.broadcasted_iota(jnp.int32, (1, 2 * LANES), 1)
    sign = jnp.where(lane < LANES, 1.0, -1.0)
    free = lax.rem(lane, LANES) >= RANK
    parts = []
    for block in range(0, STA, 2):
        rows = [z_buf[n * DAY : (n + 1) * DAY].reshape(DAY * SLOT, 2 * LANES) for n in (block, block + 1)]
        packed = dot(gather[0:ROWS], jnp.concatenate(rows, axis=1))
        parts += [packed[:, 0 : 2 * LANES], packed[:, 2 * LANES :]]
    for g in range(0, STA, GROUP):
        for n in range(GROUP - 1):
            part = jnp.where(free, pltpu.roll(parts[g + GROUP - 1], RANK - n * PIECE, 1), parts[g + n])
            at = (g // GROUP * (GROUP - 1) + n) * 2 * LANES
            left[0:ROWS, at : at + 2 * LANES] = part.astype(BF16)
            left[ROWS:, at : at + 2 * LANES] = (pltpu.roll(part, LANES, 1) * sign).astype(BF16)
    group = 4 * MINE

    for t in range(TILES):
        both = dot(left[...], table[t])
        re, im = both[0:ROWS], both[ROWS:]
        scale = jnp.minimum(lax.rsqrt(re * re + im * im), 4.0)
        done = []
        for n, part in enumerate((re, re * scale, im * scale)):
            total = part[0:group]
            for g in range(1, ROWS // group):
                total = total + part[g * group : (g + 1) * group]
            sums[t % 2, n] = total
            total = sums[t % 2, n, 0:MINE]
            for g in range(1, 4):
                total = total + sums[t % 2, n, g * MINE : (g + 1) * MINE]
            done.append(total * (1.0 / DAY))
        out_ref[:, t * LAG_TILE : (t + 1) * LAG_TILE] = done[0] * (done[1] * done[1] + done[2] * done[2])
    pltpu.make_async_copy(rest, rest, ssem).wait()


def local(spectra, pair_stations):
    bank = jnp.asarray(tables())
    anywhere = pl.BlockSpec(memory_space=pl.ANY)
    dma = pltpu.SemaphoreType.DMA
    return pl.pallas_call(
        correlate,
        name="correlate",
        out_shape=jax.ShapeDtypeStruct((MINE, LAGS), F32),
        in_specs=[anywhere] * 3,
        out_specs=pl.BlockSpec(memory_space=pltpu.VMEM),
        scratch_shapes=[
            pltpu.VMEM((STA, 2, STATIONS, WIDTH), BF16),
            pltpu.VMEM((STA, 2, ROWS), jnp.int32),
            pltpu.VMEM((STA, 2 * ROWS, STATIONS), BF16),
            pltpu.VMEM((STA, 2, ROWS, max(CHUNKS)), F32),
            pltpu.VMEM((STA, 2, ROWS, max(CHUNKS)), F32),
            pltpu.VMEM((STA, ROWS + SLOT, 2 * LANES), F32),
            pltpu.VMEM((STA, DAY, SLOT, 2 * LANES), BF16),
            pltpu.VMEM((DEVICES, SLOT, 2 * LANES), BF16),
            pltpu.VMEM((2 * ROWS, DEPTH), BF16),
            pltpu.VMEM((2, 3, 4 * MINE, LAG_TILE), F32),
            pltpu.VMEM((2 * WIDTH, 4 * LANES), BF16),
            pltpu.VMEM((DAY * SLOT, DAY * SLOT), BF16),
            pltpu.VMEM((TILES, DEPTH, LAG_TILE), BF16),
            dma((HALVES, STA)),
            dma((HALVES, STA)),
            dma((STA,)),
            dma((STA,)),
            dma((HALVES + 1,)),
            dma((TILES + 3,)),
            dma,
            dma,
        ],
        compiler_params=pltpu.CompilerParams(collective_id=0, has_side_effects=True, vmem_limit_bytes=107 << 19),
    )(spectra.reshape(2, STATIONS, BINS), pair_stations.T, bank)


def solution(mesh):
    placed = (P(None, "sta", "day", None), P("sta", None))
    return jax.shard_map(
        local, mesh=mesh, in_specs=placed, out_specs=P(("sta", "day"), None), check_vma=False
    )
```
